32 devices in a mesh: pool: 2 (over x), grp: 4 (over y, core), col: 4 (over z).
Axes of the slice: x: 2, y: 2, z: 4, core: 2. Of those that a mesh axis runs over, the one named last changes fastest.
Arguments:
- queries: bfloat16 [16, 2048], P('grp'), may hold values from -80 to 80
- fresh_kv: bfloat16 [16, 1024], P('grp'), may hold values from -6 to 6
- kv_cache: bfloat16 [16, 256, 1024], P('grp', 'col'), may hold values from -6 to 6
- lengths: int32 [16], P('grp'), may hold values from 1 to 256
- residual: bfloat16 [16, 4096], P('grp', 'col'), may hold values from -1.5 to 1.5
- out_proj: bfloat16 [2048, 4096], P(None, 'col'), may hold values from -0.125 to 0.125
- norm_gain: float32 [4096], P('col'), may hold values from 0.1 to 1.9
- router: bfloat16 [4096, 4], P('col'), may hold values from -0.09375 to 0.09375
- routes: int32 [16, 2], replicated, may hold values from 0 to 3, all different within a row; in each aligned block of 4 rows (0 to 3, 4 to 7, ...) at most 3 rows name the same one
- w_gate: bfloat16 [4096, 28672], P('col', 'grp'), may hold values from -0.09375 to 0.09375
- w_up: bfloat16 [4096, 28672], P('col', 'grp'), may hold values from -0.09375 to 0.09375
- w_down: bfloat16 [28672, 4096], P('grp', 'col'), may hold values from -0.0625 to 0.0625
Outputs:
- next_stream: bfloat16 [16, 4096], P('grp', 'col')
The draws below stay inside these ranges and needn't reach their ends.
Inputs may be any that keep to these rules, and one draw needn't show every extreme that they name: `routes`: each row names two different experts. Among the 4 rows of one grp index (aligned blocks) no expert is named by more than 3 rows, and in some blocks one expert is named by exactly 3 rows.
All inputs are finite; a program needn't handle non-finite values.
Results may differ from the reference program's by a relative error of at most 0.0075.
Values may be sent and summed in bfloat16 or wider, within the bound.
A program may use at most 128 MiB of HBM per device.

```python
import math
import jax
import jax.numpy as jnp
import numpy as np
from jax import lax

D = 4096
HEADS = 16
KV_HEADS = 4
HEAD_DIM = 128
EXPERTS = 4
INNER = 7168
ROWS_DEV = 4
CAPB = 3
ROWS = 16
CACHE = 256
CAP = 12
N_GRP = 4


def aligned_parts(key):
    sign_bits = jax.random.randint(jax.random.fold_in(key, 101), (ROWS, KV_HEADS, HEAD_DIM), 0, 2)
    signs = (2 * sign_bits - 1).astype(jnp.float32)
    offset = jax.random.randint(jax.random.fold_in(key, 102), (), 0, ROWS_DEV)
    chosen = jnp.arange(ROWS, dtype=jnp.int32) % ROWS_DEV == offset
    levels = jax.random.randint(jax.random.fold_in(key, 103), (ROWS,), 0, 3)
    target = jnp.where(levels == 0, 120.0, jnp.where(levels == 1, 200.0, 320.0))
    return (signs, chosen, target)


def draw_queries(key, part):
    signs, chosen, target = aligned_parts(key)
    key = jax.random.fold_in(key, 1)
    base = jnp.clip(jax.random.normal(key, (ROWS, HEADS * HEAD_DIM), jnp.float32), -6.0, 6.0)
    strength = target / math.sqrt(HEAD_DIM)
    repeated = jnp.repeat(signs, HEADS // KV_HEADS, axis=1).reshape(ROWS, HEADS * HEAD_DIM)
    base = jnp.where(chosen[:, None], repeated * strength[:, None], base)
    return base.astype(jnp.bfloat16)


def draw_fresh_kv(key, part):
    signs, chosen, target = aligned_parts(key)
    key = jax.random.fold_in(key, 2)
    kv_width = KV_HEADS * HEAD_DIM
    base = jnp.clip(jax.random.normal(key, (ROWS, 2 * kv_width), jnp.float32), -6.0, 6.0)
    shrink = 1.0 - 2.0 / target
    own_keys = signs.reshape(ROWS, kv_width) * shrink[:, None]
    base = jnp.concatenate([jnp.where(chosen[:, None], own_keys, base[:, :kv_width]), base[:, kv_width:]], axis=1)
    return base.astype(jnp.bfloat16)


def draw_kv_cache(key, part):
    signs, chosen, target = aligned_parts(key)
    key = jax.random.fold_in(key, 3)
    kv_width = KV_HEADS * HEAD_DIM
    base = jnp.clip(jax.random.normal(key, (ROWS, CACHE, 2 * kv_width), jnp.float32), -6.0, 6.0)
    start_keys = jnp.where(chosen[:, None], signs.reshape(ROWS, kv_width), base[:, 0, :kv_width])
    base = base.at[:, 0, :kv_width].set(start_keys)
    return base.astype(jnp.bfloat16)


def touch_ends(values, key, low, top_value):
    index_at = [jax.random.randint(jax.random.fold_in(key, axis), (), 0, length) for axis, length in enumerate(values.shape)]
    longest = values.shape.index(max(values.shape))
    next_to = index_at[:longest] + [(index_at[longest] + 1) % values.shape[longest]] + index_at[longest + 1:]
    return values.at[tuple(index_at)].set(low).at[tuple(next_to)].set(top_value)


def steps_of(stream_key, dims, split, least, largest):
    def one(position, shards_of):
        steps = jax.random.uniform(jax.random.fold_in(jax.random.fold_in(stream_key, 6), position), (shards_of,), jnp.float32, least / len(split), largest / len(split))
        return jnp.repeat(jnp.exp(steps), dims[position] // shards_of).reshape((-1,) + (1,) * (len(dims) - position - 1))

    loudness = one(*split[0])
    for cut in split[1:]:
        loudness = loudness * one(*cut)
    return loudness


def deal_out(rng, own, number, rows, number_of, top, most, skew):
    ranking = jax.random.permutation(rng, number_of)
    heavy_load, ordinary = load_shares(number_of, rows * top, most, skew, True), load_shares(number_of, rows * top, most, skew, False)
    places = jnp.arange(number_of)

    def named(sizes, turn):
        used = int((sizes > 0).sum())
        fixed = max(1, used // 4)
        shifted = fixed + (places - fixed + turn * (used - fixed)) % max(1, number_of - fixed)
        return jnp.zeros((number_of,), jnp.int32).at[ranking[jnp.where(places < fixed, places, shifted)]].set(jnp.asarray(sizes, jnp.int32))

    sizes = jnp.where(number % 4 == 0, named(heavy_load, number // 4), named(ordinary, number - number // 4 - 1))
    mixed = jax.random.permutation(jax.random.fold_in(own, 3), number_of)
    source_of, receiver = mixed[0:number_of // 2 * 2:2], mixed[1:number_of // 2 * 2:2]
    slack = jnp.minimum(sizes[source_of] - 1, most - sizes[receiver]) // 2
    slack = jnp.where((source_of == ranking[0]) | (receiver == ranking[0]) | (sizes[receiver] == 0), 0, jnp.maximum(slack, 0))
    shifted = jax.random.randint(jax.random.fold_in(own, 4), (number_of // 2,), 0, 1 << 20) % (slack + 1)
    sizes = sizes.at[source_of].add(-shifted).at[receiver].add(shifted)
    items = jnp.searchsorted(jnp.cumsum(sizes), jnp.arange(rows * top), side="right").astype(jnp.int32)
    grid = items.reshape(top, rows).T
    grid = grid[jax.random.permutation(jax.random.fold_in(own, 1), rows)]
    turn = jax.random.randint(jax.random.fold_in(own, 2), (rows, 1), 0, top)
    return jnp.take_along_axis(grid, (jnp.arange(top)[None, :] + turn) % top, axis=1)


def load_shares(number_of, total, reach, lean, full):
    weights = [(1 << 20) // math.isqrt(standing ** lean) + 1 for standing in range(1, number_of + 1)]
    largest = reach if full else min(reach, max(-(-total // number_of), total * weights[0] // sum(weights)))
    least = 1 if total - largest >= number_of - 1 else 0
    given, spare = [largest] + [least] * (number_of - 1), total - largest - least * (number_of - 1)
    while spare > 0:
        free = [i for i in range(1, number_of) if given[i] < largest] or [i for i in range(1, number_of) if given[i] < reach]
        whole, left = sum([weights[i] for i in free]), spare
        for i in free:
            addition = min(reach - given[i], max(1, left * weights[i] // whole), spare)
            given[i] = given[i] + addition
            spare = spare - addition
    return np.array(given)


def gaussian(key, shape, deviation, limit, split=(), kind=jnp.bfloat16):
    values = deviation * jax.random.normal(key, shape, jnp.float32)
    if split:
        values = values * steps_of(key, shape, split, -0.22, 0.18)
    return jnp.clip(values, -limit, limit).astype(kind)


def setup_inputs(seed: int = 0) -> dict:
    seeds = jax.random.split(jax.random.key(seed), 13)
    queries = draw_queries(jax.random.fold_in(seeds[12], 71), 0)
    fresh_kv = draw_fresh_kv(jax.random.fold_in(seeds[12], 71), 0)
    kv_cache = draw_kv_cache(jax.random.fold_in(seeds[12], 71), 0)
    lengths = touch_ends(jax.random.randint(seeds[3], (ROWS,), 1, CACHE + 1), jax.random.fold_in(seeds[3], 1), 1, CACHE).astype(jnp.int32)
    residual = gaussian(seeds[4], (ROWS, D), 0.25, 1.5, ((0, 4), (1, 4)))
    out_proj = gaussian(seeds[5], (HEADS * HEAD_DIM, D), (HEADS * HEAD_DIM) ** -0.5, 0.125, ((1, 4),))
    norm_gain = jnp.clip(1.0 + 0.18 * jax.random.normal(seeds[6], (D,), jnp.float32), 0.1, 1.9)
    router = gaussian(seeds[7], (D, EXPERTS), D ** -0.5, 0.09375, ((0, 4),))
    routes_keys = jax.random.split(jax.random.fold_in(seeds[8], 1), ROWS // ROWS_DEV)
    routes_turns = jax.random.permutation(jax.random.fold_in(seeds[8], 3), ROWS // ROWS_DEV)
    routes = jax.vmap(lambda own, number: deal_out(jax.random.fold_in(seeds[8], 2), own, number, ROWS_DEV, EXPERTS, 2, CAPB, 2))(routes_keys, routes_turns).reshape((ROWS, 2))
    w_gate = gaussian(seeds[9], (D, EXPERTS * INNER), D ** -0.5, 0.09375, ((0, 4), (1, 4)))
    w_up = gaussian(seeds[10], (D, EXPERTS * INNER), D ** -0.5, 0.09375, ((0, 4), (1, 4)))
    w_down = gaussian(seeds[11], (EXPERTS * INNER, D), INNER ** -0.5, 0.0625, ((0, 4), (1, 4)))
    return {"queries": queries, "fresh_kv": fresh_kv, "kv_cache": kv_cache, "lengths": lengths, "residual": residual, "out_proj": out_proj, "norm_gain": norm_gain, "router": router, "routes": routes, "w_gate": w_gate, "w_up": w_up, "w_down": w_down}


EPSILON = 1e-05
FLOOR_SCORE = -1e+30
FULL_PRECISION = lax.Precision.HIGHEST

def slot_tables(routes, blocks, capacity):
    row_count = routes.shape[0]
    per_block = row_count // blocks
    labels = jnp.arange(EXPERTS, dtype=jnp.int32)
    route_hits = (routes[:, :, None] == labels[None, None, :]).astype(jnp.int32)
    flat_hits = route_hits.reshape(blocks, per_block * 2, EXPERTS)
    earlier = jnp.cumsum(flat_hits, axis=1) - flat_hits
    slot_index = lax.optimization_barrier(jnp.sum(earlier * flat_hits, axis=2)).reshape(blocks, per_block, 2)
    owners = routes.reshape(blocks, per_block, 2)
    expert_hit = (owners[:, :, :, None] == labels[None, None, None, :]).astype(jnp.float32)
    slot_hit = (slot_index[:, :, :, None] == jnp.arange(capacity, dtype=jnp.int32)[None, None, None, :]).astype(jnp.float32)
    return jnp.einsum('brke,brkc->becr', expert_hit, slot_hit, precision=FULL_PRECISION)

def reference(queries, fresh_kv, kv_cache, lengths, residual, out_proj, norm_gain, router, routes, w_gate, w_up, w_down):
    group_size = HEADS // KV_HEADS
    kv_width = KV_HEADS * HEAD_DIM
    score_scale = HEAD_DIM ** (-0.5)
    query_heads = queries.astype(jnp.float32).reshape(ROWS, KV_HEADS, group_size, HEAD_DIM)
    key_part = kv_cache[:, :, :kv_width].astype(jnp.float32).reshape(ROWS, CACHE, KV_HEADS, HEAD_DIM)
    value_part = kv_cache[:, :, kv_width:].astype(jnp.float32).reshape(ROWS, CACHE, KV_HEADS, HEAD_DIM)
    new_keys = fresh_kv[:, :kv_width].astype(jnp.float32).reshape(ROWS, KV_HEADS, HEAD_DIM)
    new_values = fresh_kv[:, kv_width:].astype(jnp.float32).reshape(ROWS, KV_HEADS, HEAD_DIM)
    scores = jnp.einsum('rjgd,rpjd->rjgp', query_heads, key_part, precision=FULL_PRECISION) * score_scale
    own_score = jnp.einsum('rjgd,rjd->rjg', query_heads, new_keys, precision=FULL_PRECISION) * score_scale
    valid = (jnp.arange(CACHE, dtype=jnp.int32)[None, :] < lengths[:, None])[:, None, None, :]
    peak_score = jnp.maximum(lax.optimization_barrier(jnp.max(jnp.where(valid, scores, FLOOR_SCORE), axis=3)), own_score)
    cached_weights = jnp.where(valid, jnp.exp(scores - peak_score[..., None]), 0.0)
    own_weight = jnp.exp(own_score - peak_score)
    weight_sum = lax.optimization_barrier(jnp.sum(cached_weights, axis=3)) + own_weight
    mixed_sum = jnp.einsum('rjgp,rpjd->rjgd', cached_weights, value_part, precision=FULL_PRECISION)
    mixed_sum = mixed_sum + own_weight[..., None] * new_values[:, :, None, :]
    attended = (mixed_sum / weight_sum[..., None]).reshape(ROWS, HEADS * HEAD_DIM).astype(jnp.bfloat16)
    projected = jnp.dot(attended, out_proj, preferred_element_type=jnp.float32)
    stream = (residual.astype(jnp.float32) + projected).astype(jnp.bfloat16)
    wide = stream.astype(jnp.float32)
    scaled = (wide * norm_gain).astype(jnp.bfloat16)
    inverse = lax.rsqrt(lax.optimization_barrier(jnp.sum(wide * wide, axis=1)) / D + EPSILON)
    logits = jnp.dot(scaled, router, preferred_element_type=jnp.float32) * inverse[:, None]
    labels = jnp.arange(EXPERTS, dtype=jnp.int32)
    first_logit = lax.optimization_barrier(jnp.sum(jnp.where(routes[:, 0:1] == labels[None, :], logits, 0.0), axis=1))
    second_logit = lax.optimization_barrier(jnp.sum(jnp.where(routes[:, 1:2] == labels[None, :], logits, 0.0), axis=1))
    pair_weights = jnp.stack([jax.nn.sigmoid(first_logit - second_logit), jax.nn.sigmoid(second_logit - first_logit)], axis=1)
    tables = slot_tables(routes, N_GRP, CAPB)
    scaled_blocks = scaled.astype(jnp.float32).reshape(N_GRP, ROWS_DEV, D)
    inverse_blocks = inverse.reshape(N_GRP, ROWS_DEV)
    result = wide
    for expert in range(EXPERTS):
        table = tables[:, expert]
        slot_rows = jnp.einsum('bcr,brd->bcd', table, scaled_blocks, precision=FULL_PRECISION).reshape(CAP, D).astype(jnp.bfloat16)
        slot_inverse = jnp.einsum('bcr,br->bc', table, inverse_blocks, precision=FULL_PRECISION).reshape(CAP)
        row_weight = lax.optimization_barrier(jnp.sum(jnp.where(routes == expert, pair_weights, 0.0), axis=1)).reshape(N_GRP, ROWS_DEV)
        slot_weight = jnp.einsum('bcr,br->bc', table, row_weight, precision=FULL_PRECISION).reshape(CAP)
        gate_sum = jnp.dot(slot_rows, w_gate[:, expert * INNER:(expert + 1) * INNER], preferred_element_type=jnp.float32) * slot_inverse[:, None]
        up_sum = jnp.dot(slot_rows, w_up[:, expert * INNER:(expert + 1) * INNER], preferred_element_type=jnp.float32) * slot_inverse[:, None]
        hidden = (jax.nn.silu(gate_sum) * up_sum * slot_weight[:, None]).astype(jnp.bfloat16)
        slot_out = jnp.dot(hidden, w_down[expert * INNER:(expert + 1) * INNER, :], preferred_element_type=jnp.float32).reshape(N_GRP, CAPB, D)
        result = result + jnp.einsum('bcr,bcd->brd', table, slot_out, precision=FULL_PRECISION).reshape(ROWS, D)
    return result.astype(jnp.bfloat16)
```

```python
import jax
import jax.numpy as jnp
from jax import lax
from jax.experimental import pallas as pl
from jax.experimental.pallas import tpu as pltpu
from jax.sharding import PartitionSpec as P

D = 4096
HEADS = 16
KV_HEADS = 4
HEAD_DIM = 128
EXPERTS = 4
CAPB = 3


EPSILON = 1e-05
FLOOR_SCORE = -1e30
FULL_PRECISION = lax.Precision.HIGHEST


def merged(part, axis, combine):
    gathered = jax.tree.map(lambda a: lax.all_gather(a, axis), part)

    def take(source):
        return jax.tree.map(lambda a: lax.dynamic_index_in_dim(a, source, 0, False), gathered)

    return lax.fori_loop(
        1, lax.axis_size(axis), lambda source, state: combine(state, take(source)), take(0)
    )


def slot_tables(routes, blocks, capacity):
    row_count = routes.shape[0]
    per_block = row_count // blocks
    labels = jnp.arange(EXPERTS, dtype=jnp.int32)
    route_hits = (routes[:, :, None] == labels[None, None, :]).astype(jnp.int32)
    flat_hits = route_hits.reshape(blocks, per_block * 2, EXPERTS)
    earlier = jnp.cumsum(flat_hits, axis=1) - flat_hits
    slot_index = jnp.sum(earlier * flat_hits, axis=2).reshape(blocks, per_block, 2)
    owners = routes.reshape(blocks, per_block, 2)
    expert_hit = (owners[:, :, :, None] == labels[None, None, None, :]).astype(jnp.float32)
    slot_hit = (
        slot_index[:, :, :, None] == jnp.arange(capacity, dtype=jnp.int32)[None, None, None, :]
    ).astype(jnp.float32)
    return jnp.einsum("brke,brkc->becr", expert_hit, slot_hit, precision=FULL_PRECISION)


def attend_block(queries, kv_cache, lengths, first_pos):
    row_count = queries.shape[0]
    group_size = HEADS // KV_HEADS
    kv_width = KV_HEADS * HEAD_DIM
    positions = kv_cache.shape[1]
    query_heads = queries.reshape(row_count, KV_HEADS, group_size, HEAD_DIM)
    key_part = kv_cache[:, :, :kv_width].reshape(row_count, positions, KV_HEADS, HEAD_DIM)
    value_part = (
        kv_cache[:, :, kv_width:]
        .astype(jnp.float32)
        .reshape(row_count, positions, KV_HEADS, HEAD_DIM)
    )
    scores = jnp.einsum(
        "rjgd,rpjd->rjgp", query_heads, key_part, preferred_element_type=jnp.float32
    ) * HEAD_DIM ** (-0.5)
    place = first_pos + jnp.arange(positions, dtype=jnp.int32)
    valid = (place[None, :] < lengths[:, None])[:, None, None, :]
    peak_score = jnp.max(jnp.where(valid, scores, FLOOR_SCORE), axis=3)
    cached_weights = jnp.where(valid, jnp.exp(scores - peak_score[..., None]), 0.0)
    weight_sum = jnp.sum(cached_weights, axis=3)
    mixed_sum = jnp.einsum("rjgp,rpjd->rjgd", cached_weights, value_part, precision=FULL_PRECISION)
    return (
        peak_score.reshape(row_count, HEADS),
        weight_sum.reshape(row_count, HEADS),
        mixed_sum.reshape(row_count, HEADS, HEAD_DIM),
    )


def skip_block(queries, kv_cache, lengths, first_pos):
    row_count = queries.shape[0]
    return (
        jnp.full((row_count, HEADS), FLOOR_SCORE, jnp.float32),
        jnp.zeros((row_count, HEADS), jnp.float32),
        jnp.zeros((row_count, HEADS, HEAD_DIM), jnp.float32),
    )


def merge_states(earlier_state, later_state):
    peak_first, sum_first, mixed_first = earlier_state
    peak_second, sum_second, mixed_second = later_state
    peak_both = jnp.maximum(peak_first, peak_second)
    scale_first = jnp.exp(peak_first - peak_both)
    scale_second = jnp.exp(peak_second - peak_both)
    return (
        peak_both,
        sum_first * scale_first + sum_second * scale_second,
        mixed_first * scale_first[..., None] + mixed_second * scale_second[..., None],
    )


def fold_own(queries, fresh_kv, peak_score, weight_sum, mixed_sum):
    row_count = queries.shape[0]
    group_size = HEADS // KV_HEADS
    kv_width = KV_HEADS * HEAD_DIM
    query_heads = queries.reshape(row_count, KV_HEADS, group_size, HEAD_DIM)
    new_keys = fresh_kv[:, :kv_width].reshape(row_count, KV_HEADS, HEAD_DIM)
    new_values = fresh_kv[:, kv_width:].astype(jnp.float32).reshape(row_count, KV_HEADS, HEAD_DIM)
    own_score = jnp.einsum(
        "rjgd,rjd->rjg", query_heads, new_keys, preferred_element_type=jnp.float32
    ) * HEAD_DIM ** (-0.5)
    own_score = own_score.reshape(row_count, HEADS)
    peak_both = jnp.maximum(peak_score, own_score)
    old_scale = jnp.exp(peak_score - peak_both)
    own_weight = jnp.exp(own_score - peak_both)
    total_weight = weight_sum * old_scale + own_weight
    spread_values = jnp.repeat(new_values, group_size, axis=1)
    mixed_total = mixed_sum * old_scale[..., None] + own_weight[..., None] * spread_values
    return (
        (mixed_total / total_weight[..., None])
        .reshape(row_count, HEADS * HEAD_DIM)
        .astype(jnp.bfloat16)
    )


def expert_inputs(slot_rows, norm_gain, router, w_gate, w_up):
    scaled = (slot_rows.astype(jnp.float32) * norm_gain).astype(jnp.bfloat16)
    gate_part = jnp.dot(scaled, w_gate, preferred_element_type=jnp.float32)
    up_part = jnp.dot(scaled, w_up, preferred_element_type=jnp.float32)
    wide_rows = slot_rows.astype(jnp.float32)
    square_part = jnp.sum(wide_rows * wide_rows, axis=1)
    logit_part = jnp.dot(scaled, router, preferred_element_type=jnp.float32)
    return (gate_part, up_part, square_part, logit_part)


def no_inputs(slot_rows, norm_gain, router, w_gate, w_up):
    slot_count = slot_rows.shape[0]
    return (
        jnp.zeros((slot_count, w_gate.shape[1]), jnp.float32),
        jnp.zeros((slot_count, w_up.shape[1]), jnp.float32),
        jnp.zeros((slot_count,), jnp.float32),
        jnp.zeros((slot_count, router.shape[1]), jnp.float32),
    )


def activate(gate_sum, up_sum, squares, logit_sum, slot_rival, expert_id):
    inverse = lax.rsqrt(squares / D + EPSILON)
    labels = jnp.arange(EXPERTS, dtype=jnp.int32)
    logits = logit_sum * inverse[:, None]
    own_logit = jnp.sum(jnp.where(labels[None, :] == expert_id, logits, 0.0), axis=1)
    rival_logit = jnp.sum(
        jnp.where(labels.astype(jnp.float32)[None, :] == slot_rival[:, None], logits, 0.0), axis=1
    )
    slot_weight = jax.nn.sigmoid(own_logit - rival_logit)
    gate_scaled = gate_sum * inverse[:, None]
    up_scaled = up_sum * inverse[:, None]
    return (jax.nn.silu(gate_scaled) * up_scaled * slot_weight[:, None]).astype(jnp.bfloat16)


def expert_down(hidden, w_down):
    return jnp.dot(hidden, w_down, preferred_element_type=jnp.float32)


def no_down(hidden, w_down):
    return jnp.zeros((hidden.shape[0], w_down.shape[1]), jnp.float32)


def local(
    queries,
    fresh_kv,
    kv_cache,
    lengths,
    residual,
    out_proj,
    norm_gain,
    router,
    routes,
    w_gate,
    w_up,
    w_down,
):
    group_count = lax.axis_size("grp")
    group_index = lax.axis_index("grp")
    col_index = lax.axis_index("col")
    attention_side = lax.axis_index("pool") == 0
    feature_count = residual.shape[1]
    first_pos = col_index * kv_cache.shape[1]
    states = lax.cond(
        attention_side, attend_block, skip_block, queries, kv_cache, lengths, first_pos
    )
    peak_score, weight_sum, mixed_sum = merged(states, "col", merge_states)
    attended = fold_own(queries, fresh_kv, peak_score, weight_sum, mixed_sum)
    projected = jnp.dot(attended, out_proj, preferred_element_type=jnp.float32)
    stream = (residual.astype(jnp.float32) + projected).astype(jnp.bfloat16)
    tables = slot_tables(routes, group_count, CAPB)
    copies = group_count // EXPERTS
    expert_id = group_index // copies
    own_table = lax.dynamic_index_in_dim(tables, group_index, 0, keepdims=False)
    expert_table = lax.dynamic_index_in_dim(tables, expert_id, 1, keepdims=False)
    placed = jnp.einsum(
        "ecr,rd->ecd", own_table.astype(jnp.bfloat16), stream, preferred_element_type=jnp.float32
    )
    filled = jnp.where(
        attention_side,
        jnp.repeat(placed.astype(jnp.bfloat16), copies, axis=0),
        jnp.zeros((group_count, CAPB, feature_count), jnp.bfloat16),
    )
    outgoing = jnp.concatenate([jnp.zeros_like(filled), filled], axis=0)
    gathered = lax.all_to_all(outgoing, ("pool", "grp"), split_axis=0, concat_axis=0, tiled=True)[
        :group_count
    ]
    slot_rows = gathered.reshape(group_count * CAPB, feature_count)
    rival_rows = (jnp.sum(routes, axis=1).reshape(group_count, -1) - expert_id).astype(jnp.float32)
    slot_rival = jnp.einsum(
        "bcr,br->bc", expert_table, rival_rows, precision=FULL_PRECISION
    ).reshape(-1)
    partials = lax.cond(
        attention_side, no_inputs, expert_inputs, slot_rows, norm_gain, router, w_gate, w_up
    )
    gate_sum, up_sum, squares, logit_sum = lax.psum(partials, "col")
    hidden = activate(gate_sum, up_sum, squares, logit_sum, slot_rival, expert_id)
    slot_out = lax.cond(attention_side, no_down, expert_down, hidden, w_down)
    returned = jnp.einsum(
        "bcr,bcd->brd",
        expert_table,
        slot_out.reshape(group_count, CAPB, feature_count),
        precision=FULL_PRECISION,
    )
    block_ids = jnp.arange(group_count, dtype=jnp.int32)
    own_pieces = jnp.where(
        (block_ids == group_index)[:, None, None], stream.astype(jnp.float32)[None, :, :], 0.0
    )
    pieces = jnp.where(attention_side, own_pieces, returned)
    outgoing_back = jnp.concatenate([pieces, pieces], axis=0)
    received = lax.all_to_all(
        outgoing_back, ("pool", "grp"), split_axis=0, concat_axis=0, tiled=True
    )
    return jnp.sum(received, axis=0).astype(jnp.bfloat16)

MESH = pl.DeviceIdType.MESH


def fused_kernel(
    queries,
    fresh,
    kv_hbm,
    lengths,
    residual,
    proj_hbm,
    gain,
    router,
    routes,
    gate_hbm,
    up_hbm,
    down_hbm,
    out,
    kv,
    proj,
    gate_w,
    up_w,
    down_w,
    query_rows,
    key_rows,
    value_rows,
    mixed_own,
    stat_own,
    mixed_in,
    stat_in,
    attended_rows,
    streams,
    sums_own,
    sums_in,
    part_send,
    part_in,
    hidden_own,
    hidden_in,
    pieces,
    returned,
    load_sem,
    weight_sem,
    send_a,
    recv_a,
    send_b,
    recv_b,
    send_c,
    recv_c,
    send_d,
    recv_d,
    send_e,
    recv_e,
    send_f,
    recv_f,
    send_g,
    recv_g,
):
    pools = lax.axis_size("pool")
    groups = lax.axis_size("grp")
    cols = lax.axis_size("col")
    pool = lax.axis_index("pool")
    grp = lax.axis_index("grp")
    col = lax.axis_index("col")
    rows = queries.shape[0]
    positions = kv.shape[1]
    kv_width = KV_HEADS * HEAD_DIM
    group_size = HEADS // KV_HEADS
    chunk = gate_w.shape[2]
    states = rows * HEADS
    first_column = pool * (chunk * cols)

    loads = [
        pltpu.make_async_copy(kv_hbm, kv, load_sem.at[0]),
        pltpu.make_async_copy(proj_hbm, proj, load_sem.at[1]),
    ]
    for load in loads:
        load.start()
    steps = list(range(1, cols)) + [0]
    gate_loads, up_loads, down_loads = {}, {}, {}
    for k in steps:
        owner = lax.rem(col + k, cols)
        window = pl.ds(pl.multiple_of(first_column + owner * chunk, 128), chunk)
        gate_loads[k] = pltpu.make_async_copy(
            gate_hbm.at[:, window], gate_w.at[k], weight_sem.at[0, k]
        )
        up_loads[k] = pltpu.make_async_copy(up_hbm.at[:, window], up_w.at[k], weight_sem.at[1, k])
        gate_loads[k].start()
        up_loads[k].start()
    for k in range(cols):
        source = lax.rem(col + cols - k, cols)
        window = pl.ds(pl.multiple_of(first_column + source * chunk, 128), chunk)
        down_loads[k] = pltpu.make_async_copy(
            down_hbm.at[window, :], down_w.at[k], weight_sem.at[2, k]
        )
        down_loads[k].start()

    def col_peer(k):
        return (pool, grp, lax.rem(col + k, cols))

    def row_peer(kp, kg):
        return (lax.rem(pool + kp, pools), lax.rem(grp + kg, groups), col)

    row_steps = [(kp, kg) for kg in range(groups) for kp in range(pools) if kp or kg]
    barrier = pltpu.get_barrier_semaphore()
    for k in range(1, cols):
        pl.semaphore_signal(barrier, inc=1, device_id=col_peer(k), device_id_type=MESH)
    for kp, kg in row_steps:
        pl.semaphore_signal(barrier, inc=1, device_id=row_peer(kp, kg), device_id_type=MESH)

    wide_queries = queries[...].astype(jnp.float32)
    wide_fresh = fresh[...].astype(jnp.float32)
    for h in range(HEADS):
        j = h // group_size
        place = pl.ds(h, rows, stride=HEADS)
        query_rows[place, :] = wide_queries[:, h * HEAD_DIM : (h + 1) * HEAD_DIM]
        key_rows[place, :] = wide_fresh[:, j * HEAD_DIM : (j + 1) * HEAD_DIM]
        value_rows[place, :] = wide_fresh[
            :, kv_width + j * HEAD_DIM : kv_width + (j + 1) * HEAD_DIM
        ]
    scale = HEAD_DIM ** (-0.5)
    own_score = jnp.sum(query_rows[...] * key_rows[...], axis=1, keepdims=True) * scale
    head_of = lax.broadcasted_iota(jnp.int32, (HEADS, HEAD_DIM), 0) // group_size
    place = col * positions + lax.broadcasted_iota(jnp.int32, (HEADS, positions), 1)
    loads[0].wait()
    peaks, totals = [], []
    for r in range(rows):
        head_rows = query_rows[r * HEADS : (r + 1) * HEADS, :]
        spread = jnp.concatenate(
            [jnp.where(head_of == j, head_rows, 0.0) for j in range(KV_HEADS)], axis=1
        ).astype(jnp.bfloat16)
        scores = (
            lax.dot_general(
                spread,
                kv[r, :, :kv_width],
                (((1,), (1,)), ((), ())),
                preferred_element_type=jnp.float32,
            )
            * scale
        )
        valid = place < lengths[r]
        peak = jnp.max(jnp.where(valid, scores, FLOOR_SCORE), axis=1, keepdims=True)
        weights = jnp.where(valid, jnp.exp(scores - peak), 0.0)
        total = jnp.sum(weights, axis=1, keepdims=True)
        high = weights.astype(jnp.bfloat16)
        low = (weights - high.astype(jnp.float32)).astype(jnp.bfloat16)
        values = kv[r, :, kv_width:]
        product = jnp.dot(high, values, preferred_element_type=jnp.float32) + jnp.dot(
            low, values, preferred_element_type=jnp.float32
        )
        mixed = jnp.zeros((HEADS, HEAD_DIM), jnp.float32)
        for j in range(KV_HEADS):
            mixed = mixed + jnp.where(
                head_of == j, product[:, j * HEAD_DIM : (j + 1) * HEAD_DIM], 0.0
            )
        mixed = mixed / jnp.where(total > 0.0, total, 1.0)
        mixed_own[r * HEADS : (r + 1) * HEADS, :] = mixed.astype(jnp.bfloat16)
        peaks.append(peak)
        totals.append(total)
    peak = jnp.concatenate(peaks, axis=0)
    total = jnp.concatenate(totals, axis=0)
    diagonal = lax.broadcasted_iota(jnp.int32, (states, 128), 0) == lax.broadcasted_iota(
        jnp.int32, (states, 128), 1
    )
    stat_own[...] = jnp.zeros_like(stat_own)
    stat_own[0:1, :] = jnp.sum(jnp.where(diagonal, peak, 0.0), axis=0, keepdims=True)
    stat_own[1:2, :] = jnp.sum(jnp.where(diagonal, total, 0.0), axis=0, keepdims=True)

    pl.semaphore_wait(barrier, cols - 1 + len(row_steps))
    state_copies = []
    for k in range(1, cols):
        for src, dst, send, recv in (
            (stat_own, stat_in, send_b, recv_b),
            (mixed_own, mixed_in, send_a, recv_a),
        ):
            copy = pltpu.make_async_remote_copy(
                src_ref=src,
                dst_ref=dst.at[k - 1],
                send_sem=send.at[k - 1],
                recv_sem=recv.at[k - 1],
                device_id=col_peer(k),
                device_id_type=MESH,
            )
            copy.start()
            state_copies.append(copy)
    for copy in state_copies:
        copy.wait()

    all_peaks, all_totals = [peak], [total]
    for k in range(1, cols):
        all_peaks.append(
            jnp.sum(jnp.where(diagonal, stat_in[k - 1, 0:1, :], 0.0), axis=1, keepdims=True)
        )
        all_totals.append(
            jnp.sum(jnp.where(diagonal, stat_in[k - 1, 1:2, :], 0.0), axis=1, keepdims=True)
        )
    top = own_score
    for other in all_peaks:
        top = jnp.maximum(top, other)
    own_weight = jnp.exp(own_score - top)
    weight_sum = own_weight
    mixed_sum = own_weight * value_rows[...]
    for k in range(cols):
        part = mixed_own[...] if k == 0 else mixed_in[k - 1]
        weight = all_totals[k] * jnp.exp(all_peaks[k] - top)
        weight_sum = weight_sum + weight
        mixed_sum = mixed_sum + weight * part.astype(jnp.float32)
    attended_rows[...] = mixed_sum / weight_sum
    attended = jnp.concatenate(
        [attended_rows[pl.ds(h, rows, stride=HEADS), :] for h in range(HEADS)], axis=1
    ).astype(jnp.bfloat16)
    loads[1].wait()
    projected = jnp.dot(attended, proj[...], preferred_element_type=jnp.float32)
    stream = (residual[...].astype(jnp.float32) + projected).astype(jnp.bfloat16)
    streams[grp] = stream.astype(jnp.float32)

    stream_copies = []
    for kg in range(1, groups):
        copy = pltpu.make_async_remote_copy(
            src_ref=streams.at[grp],
            dst_ref=streams.at[grp],
            send_sem=send_c.at[kg - 1],
            recv_sem=recv_c.at[kg - 1],
            device_id=row_peer(0, kg),
            device_id_type=MESH,
        )
        copy.start()
        stream_copies.append(copy)
    for copy in stream_copies:
        copy.wait()

    wide = jnp.concatenate([streams[g] for g in range(groups)], axis=0)
    scaled = (wide * gain[...]).astype(jnp.bfloat16)
    squares = jnp.sum(wide * wide, axis=1, keepdims=True)
    logit_part = lax.dot_general(
        scaled, router[...], (((1,), (1,)), ((), ())), preferred_element_type=jnp.float32
    )
    lane = lax.broadcasted_iota(jnp.int32, sums_own.shape, 1)
    packed = jnp.where(lane == EXPERTS, squares, 0.0)
    for j in range(EXPERTS):
        packed = packed + jnp.where(lane == j, logit_part[:, j : j + 1], 0.0)
    sums_own[...] = packed
    part_copies = []
    for k in range(1, cols):
        copy = pltpu.make_async_remote_copy(
            src_ref=sums_own,
            dst_ref=sums_in.at[k - 1],
            send_sem=send_d.at[k - 1],
            recv_sem=recv_d.at[k - 1],
            device_id=col_peer(k),
            device_id_type=MESH,
        )
        copy.start()
        part_copies.append(copy)
    row_count = rows * groups
    for k in steps:
        gate_loads[k].wait()
        gate_part = jnp.dot(scaled, gate_w[k], preferred_element_type=jnp.float32)
        up_loads[k].wait()
        up_part = jnp.dot(scaled, up_w[k], preferred_element_type=jnp.float32)
        if k == 0:
            break
        part_send[k - 1, :row_count, :] = gate_part.astype(jnp.bfloat16)
        part_send[k - 1, row_count:, :] = up_part.astype(jnp.bfloat16)
        copy = pltpu.make_async_remote_copy(
            src_ref=part_send.at[k - 1],
            dst_ref=part_in.at[k - 1],
            send_sem=send_e.at[k - 1],
            recv_sem=recv_e.at[k - 1],
            device_id=col_peer(k),
            device_id_type=MESH,
        )
        copy.start()
        part_copies.append(copy)

    for copy in part_copies[: cols - 1]:
        copy.wait()
    sums = sums_own[...]
    for k in range(1, cols):
        sums = sums + sums_in[k - 1]
    inverse = lax.rsqrt(sums[:, EXPERTS : EXPERTS + 1] / D + EPSILON)
    expert = grp // (groups // EXPERTS)
    square = (row_count, row_count)
    row_diagonal = lax.broadcasted_iota(jnp.int32, square, 0) == lax.broadcasted_iota(
        jnp.int32, square, 1
    )
    named = routes[...].astype(jnp.float32)
    first = jnp.sum(jnp.where(row_diagonal, named[0:1, :], 0.0), axis=1, keepdims=True)
    second = jnp.sum(jnp.where(row_diagonal, named[1:2, :], 0.0), axis=1, keepdims=True)
    expert_label = expert.astype(jnp.float32)
    chosen = jnp.logical_or(first == expert_label, second == expert_label)
    rival = first + second - expert_label
    own_logit = jnp.zeros_like(inverse)
    rival_logit = jnp.zeros_like(inverse)
    for j in range(EXPERTS):
        logit = sums[:, j : j + 1] * inverse
        own_logit = own_logit + jnp.where(expert_label == float(j), logit, 0.0)
        rival_logit = rival_logit + jnp.where(rival == float(j), logit, 0.0)
    row_weight = jnp.where(chosen, 1.0 / (1.0 + jnp.exp(rival_logit - own_logit)), 0.0)

    for copy in part_copies[cols - 1 :]:
        copy.wait()
    for k in range(1, cols):
        gate_part = gate_part + part_in[k - 1, :row_count, :].astype(jnp.float32)
        up_part = up_part + part_in[k - 1, row_count:, :].astype(jnp.float32)
    gate = gate_part * inverse
    up = up_part * inverse
    hidden = (gate / (1.0 + jnp.exp(-gate)) * up * row_weight).astype(jnp.bfloat16)
    hidden_own[...] = hidden
    hidden_copies = []
    for k in range(1, cols):
        copy = pltpu.make_async_remote_copy(
            src_ref=hidden_own,
            dst_ref=hidden_in.at[k - 1],
            send_sem=send_f.at[k - 1],
            recv_sem=recv_f.at[k - 1],
            device_id=col_peer(k),
            device_id_type=MESH,
        )
        copy.start()
        hidden_copies.append(copy)
    down_loads[0].wait()
    result = jnp.dot(hidden, down_w[0], preferred_element_type=jnp.float32)
    for k in range(1, cols):
        hidden_copies[k - 1].wait()
        down_loads[k].wait()
        result = result + jnp.dot(hidden_in[k - 1], down_w[k], preferred_element_type=jnp.float32)
    for g in range(groups):
        pieces[g] = result[g * rows : (g + 1) * rows, :]
    me = pool * groups + grp
    returned[me] = pieces[grp]
    piece_copies = []
    for i, (kp, kg) in enumerate(row_steps):
        target = row_peer(kp, kg)
        copy = pltpu.make_async_remote_copy(
            src_ref=pieces.at[target[1]],
            dst_ref=returned.at[me],
            send_sem=send_g.at[i],
            recv_sem=recv_g.at[i],
            device_id=target,
            device_id_type=MESH,
        )
        copy.start()
        piece_copies.append(copy)
    for copy in piece_copies:
        copy.wait()
    final = stream.astype(jnp.float32)
    for i in range(pools * groups):
        final = final + returned[i]
    out[...] = final.astype(jnp.bfloat16)


def fused_local(
    queries,
    fresh_kv,
    kv_cache,
    lengths,
    residual,
    out_proj,
    norm_gain,
    router,
    routes,
    w_gate,
    w_up,
    w_down,
):
    pools, groups, cols = (lax.axis_size(a) for a in ("pool", "grp", "col"))
    rows, features = residual.shape
    row_count = rows * groups
    chunk = w_gate.shape[1] // (pools * cols)
    states = rows * HEADS
    f32, bf16 = jnp.float32, jnp.bfloat16
    vmem, anywhere = pl.BlockSpec(memory_space=pltpu.VMEM), pl.BlockSpec(memory_space=pl.ANY)
    scalars = pl.BlockSpec(memory_space=pltpu.SMEM)
    peers = cols - 1
    row_peers = pools * groups - 1
    dma = pltpu.SemaphoreType.DMA
    return pl.pallas_call(
        fused_kernel,
        out_shape=jax.ShapeDtypeStruct((rows, features), bf16),
        in_specs=[
            vmem, vmem, anywhere, scalars, vmem, anywhere,
            vmem, vmem, vmem, anywhere, anywhere, anywhere,
        ],
        out_specs=vmem,
        scratch_shapes=[
            pltpu.VMEM(kv_cache.shape, bf16),
            pltpu.VMEM(out_proj.shape, bf16),
            pltpu.VMEM((cols, features, chunk), bf16),
            pltpu.VMEM((cols, features, chunk), bf16),
            pltpu.VMEM((cols, chunk, features), bf16),
            pltpu.VMEM((states, HEAD_DIM), f32),
            pltpu.VMEM((states, HEAD_DIM), f32),
            pltpu.VMEM((states, HEAD_DIM), f32),
            pltpu.VMEM((states, HEAD_DIM), bf16),
            pltpu.VMEM((8, 128), f32),
            pltpu.VMEM((peers, states, HEAD_DIM), bf16),
            pltpu.VMEM((peers, 8, 128), f32),
            pltpu.VMEM((states, HEAD_DIM), f32),
            pltpu.VMEM((groups, rows, features), f32),
            pltpu.VMEM((row_count, 128), f32),
            pltpu.VMEM((peers, row_count, 128), f32),
            pltpu.VMEM((peers, 2 * row_count, chunk), bf16),
            pltpu.VMEM((peers, 2 * row_count, chunk), bf16),
            pltpu.VMEM((row_count, chunk), bf16),
            pltpu.VMEM((peers, row_count, chunk), bf16),
            pltpu.VMEM((groups, rows, features), f32),
            pltpu.VMEM((pools * groups, rows, features), f32),
            dma((2,)),
            dma((3, cols)),
            dma((peers,)), dma((peers,)),
            dma((peers,)), dma((peers,)),
            dma((groups - 1,)), dma((groups - 1,)),
            dma((peers,)), dma((peers,)),
            dma((peers,)), dma((peers,)),
            dma((peers,)), dma((peers,)),
            dma((row_peers,)), dma((row_peers,)),
        ],
        compiler_params=pltpu.CompilerParams(
            collective_id=0, has_side_effects=True, vmem_limit_bytes=48 * 2**20
        ),
    )(
        queries,
        fresh_kv,
        kv_cache,
        lengths,
        residual,
        out_proj,
        norm_gain.reshape(1, -1),
        router.T,
        routes.T,
        w_gate,
        w_up,
        w_down,
    )


def fits_kernel(mesh, w_gate, residual):
    sizes = dict(mesh.shape)
    chunk, left = divmod(w_gate.shape[1], sizes["grp"] * sizes["pool"] * sizes["col"])
    states = residual.shape[0] // sizes["grp"] * HEADS
    return (
        left == 0
        and chunk % 128 == 0
        and residual.shape[0] % 16 == 0
        and residual.shape[0] <= 128
        and states <= 128
        and sizes["grp"] % EXPERTS == 0
    )


def solution(mesh):
    placed = (
        P("grp", None),
        P("grp", None),
        P("grp", "col", None),
        P("grp"),
        P("grp", "col"),
        P(None, "col"),
        P("col"),
        P("col", None),
        P(),
        P("col", "grp"),
        P("col", "grp"),
        P("grp", "col"),
    )

    def whole(*args):
        body = fused_local if fits_kernel(mesh, args[9], args[4]) else local
        return jax.shard_map(
            body, mesh=mesh, in_specs=placed, out_specs=P("grp", "col"), check_vma=False
        )(*args)

    return whole
```

```python
import jax
import jax.numpy as jnp
from jax import lax
from jax.experimental import pallas as pl
from jax.experimental.pallas import tpu as pltpu
from jax.sharding import PartitionSpec as P

D = 4096
HEADS = 16
KV_HEADS = 4
HEAD_DIM = 128
EXPERTS = 4
CAPB = 3


EPSILON = 1e-05
FLOOR_SCORE = -1e30
FULL_PRECISION = lax.Precision.HIGHEST


def merged(part, axis, combine):
    gathered = jax.tree.map(lambda a: lax.all_gather(a, axis), part)

    def take(source):
        return jax.tree.map(lambda a: lax.dynamic_index_in_dim(a, source, 0, False), gathered)

    return lax.fori_loop(
        1, lax.axis_size(axis), lambda source, state: combine(state, take(source)), take(0)
    )


def slot_tables(routes, blocks, capacity):
    row_count = routes.shape[0]
    per_block = row_count // blocks
    labels = jnp.arange(EXPERTS, dtype=jnp.int32)
    route_hits = (routes[:, :, None] == labels[None, None, :]).astype(jnp.int32)
    flat_hits = route_hits.reshape(blocks, per_block * 2, EXPERTS)
    earlier = jnp.cumsum(flat_hits, axis=1) - flat_hits
    slot_index = jnp.sum(earlier * flat_hits, axis=2).reshape(blocks, per_block, 2)
    owners = routes.reshape(blocks, per_block, 2)
    expert_hit = (owners[:, :, :, None] == labels[None, None, None, :]).astype(jnp.float32)
    slot_hit = (
        slot_index[:, :, :, None] == jnp.arange(capacity, dtype=jnp.int32)[None, None, None, :]
    ).astype(jnp.float32)
    return jnp.einsum("brke,brkc->becr", expert_hit, slot_hit, precision=FULL_PRECISION)


def attend_block(queries, kv_cache, lengths, first_pos):
    row_count = queries.shape[0]
    group_size = HEADS // KV_HEADS
    kv_width = KV_HEADS * HEAD_DIM
    positions = kv_cache.shape[1]
    query_heads = queries.reshape(row_count, KV_HEADS, group_size, HEAD_DIM)
    key_part = kv_cache[:, :, :kv_width].reshape(row_count, positions, KV_HEADS, HEAD_DIM)
    value_part = (
        kv_cache[:, :, kv_width:]
        .astype(jnp.float32)
        .reshape(row_count, positions, KV_HEADS, HEAD_DIM)
    )
    scores = jnp.einsum(
        "rjgd,rpjd->rjgp", query_heads, key_part, preferred_element_type=jnp.float32
    ) * HEAD_DIM ** (-0.5)
    place = first_pos + jnp.arange(positions, dtype=jnp.int32)
    valid = (place[None, :] < lengths[:, None])[:, None, None, :]
    peak_score = jnp.max(jnp.where(valid, scores, FLOOR_SCORE), axis=3)
    cached_weights = jnp.where(valid, jnp.exp(scores - peak_score[..., None]), 0.0)
    weight_sum = jnp.sum(cached_weights, axis=3)
    mixed_sum = jnp.einsum("rjgp,rpjd->rjgd", cached_weights, value_part, precision=FULL_PRECISION)
    return (
        peak_score.reshape(row_count, HEADS),
        weight_sum.reshape(row_count, HEADS),
        mixed_sum.reshape(row_count, HEADS, HEAD_DIM),
    )


def skip_block(queries, kv_cache, lengths, first_pos):
    row_count = queries.shape[0]
    return (
        jnp.full((row_count, HEADS), FLOOR_SCORE, jnp.float32),
        jnp.zeros((row_count, HEADS), jnp.float32),
        jnp.zeros((row_count, HEADS, HEAD_DIM), jnp.float32),
    )


def merge_states(earlier_state, later_state):
    peak_first, sum_first, mixed_first = earlier_state
    peak_second, sum_second, mixed_second = later_state
    peak_both = jnp.maximum(peak_first, peak_second)
    scale_first = jnp.exp(peak_first - peak_both)
    scale_second = jnp.exp(peak_second - peak_both)
    return (
        peak_both,
        sum_first * scale_first + sum_second * scale_second,
        mixed_first * scale_first[..., None] + mixed_second * scale_second[..., None],
    )


def fold_own(queries, fresh_kv, peak_score, weight_sum, mixed_sum):
    row_count = queries.shape[0]
    group_size = HEADS // KV_HEADS
    kv_width = KV_HEADS * HEAD_DIM
    query_heads = queries.reshape(row_count, KV_HEADS, group_size, HEAD_DIM)
    new_keys = fresh_kv[:, :kv_width].reshape(row_count, KV_HEADS, HEAD_DIM)
    new_values = fresh_kv[:, kv_width:].astype(jnp.float32).reshape(row_count, KV_HEADS, HEAD_DIM)
    own_score = jnp.einsum(
        "rjgd,rjd->rjg", query_heads, new_keys, preferred_element_type=jnp.float32
    ) * HEAD_DIM ** (-0.5)
    own_score = own_score.reshape(row_count, HEADS)
    peak_both = jnp.maximum(peak_score, own_score)
    old_scale = jnp.exp(peak_score - peak_both)
    own_weight = jnp.exp(own_score - peak_both)
    total_weight = weight_sum * old_scale + own_weight
    spread_values = jnp.repeat(new_values, group_size, axis=1)
    mixed_total = mixed_sum * old_scale[..., None] + own_weight[..., None] * spread_values
    return (
        (mixed_total / total_weight[..., None])
        .reshape(row_count, HEADS * HEAD_DIM)
        .astype(jnp.bfloat16)
    )


def expert_inputs(slot_rows, norm_gain, router, w_gate, w_up):
    scaled = (slot_rows.astype(jnp.float32) * norm_gain).astype(jnp.bfloat16)
    gate_part = jnp.dot(scaled, w_gate, preferred_element_type=jnp.float32)
    up_part = jnp.dot(scaled, w_up, preferred_element_type=jnp.float32)
    wide_rows = slot_rows.astype(jnp.float32)
    square_part = jnp.sum(wide_rows * wide_rows, axis=1)
    logit_part = jnp.dot(scaled, router, preferred_element_type=jnp.float32)
    return (gate_part, up_part, square_part, logit_part)


def no_inputs(slot_rows, norm_gain, router, w_gate, w_up):
    slot_count = slot_rows.shape[0]
    return (
        jnp.zeros((slot_count, w_gate.shape[1]), jnp.float32),
        jnp.zeros((slot_count, w_up.shape[1]), jnp.float32),
        jnp.zeros((slot_count,), jnp.float32),
        jnp.zeros((slot_count, router.shape[1]), jnp.float32),
    )


def activate(gate_sum, up_sum, squares, logit_sum, slot_rival, expert_id):
    inverse = lax.rsqrt(squares / D + EPSILON)
    labels = jnp.arange(EXPERTS, dtype=jnp.int32)
    logits = logit_sum * inverse[:, None]
    own_logit = jnp.sum(jnp.where(labels[None, :] == expert_id, logits, 0.0), axis=1)
    rival_logit = jnp.sum(
        jnp.where(labels.astype(jnp.float32)[None, :] == slot_rival[:, None], logits, 0.0), axis=1
    )
    slot_weight = jax.nn.sigmoid(own_logit - rival_logit)
    gate_scaled = gate_sum * inverse[:, None]
    up_scaled = up_sum * inverse[:, None]
    return (jax.nn.silu(gate_scaled) * up_scaled * slot_weight[:, None]).astype(jnp.bfloat16)


def expert_down(hidden, w_down):
    return jnp.dot(hidden, w_down, preferred_element_type=jnp.float32)


def no_down(hidden, w_down):
    return jnp.zeros((hidden.shape[0], w_down.shape[1]), jnp.float32)


def local(
    queries,
    fresh_kv,
    kv_cache,
    lengths,
    residual,
    out_proj,
    norm_gain,
    router,
    routes,
    w_gate,
    w_up,
    w_down,
):
    group_count = lax.axis_size("grp")
    group_index = lax.axis_index("grp")
    col_index = lax.axis_index("col")
    attention_side = lax.axis_index("pool") == 0
    feature_count = residual.shape[1]
    first_pos = col_index * kv_cache.shape[1]
    states = lax.cond(
        attention_side, attend_block, skip_block, queries, kv_cache, lengths, first_pos
    )
    peak_score, weight_sum, mixed_sum = merged(states, "col", merge_states)
    attended = fold_own(queries, fresh_kv, peak_score, weight_sum, mixed_sum)
    projected = jnp.dot(attended, out_proj, preferred_element_type=jnp.float32)
    stream = (residual.astype(jnp.float32) + projected).astype(jnp.bfloat16)
    tables = slot_tables(routes, group_count, CAPB)
    copies = group_count // EXPERTS
    expert_id = group_index // copies
    own_table = lax.dynamic_index_in_dim(tables, group_index, 0, keepdims=False)
    expert_table = lax.dynamic_index_in_dim(tables, expert_id, 1, keepdims=False)
    placed = jnp.einsum(
        "ecr,rd->ecd", own_table.astype(jnp.bfloat16), stream, preferred_element_type=jnp.float32
    )
    filled = jnp.where(
        attention_side,
        jnp.repeat(placed.astype(jnp.bfloat16), copies, axis=0),
        jnp.zeros((group_count, CAPB, feature_count), jnp.bfloat16),
    )
    outgoing = jnp.concatenate([jnp.zeros_like(filled), filled], axis=0)
    gathered = lax.all_to_all(outgoing, ("pool", "grp"), split_axis=0, concat_axis=0, tiled=True)[
        :group_count
    ]
    slot_rows = gathered.reshape(group_count * CAPB, feature_count)
    rival_rows = (jnp.sum(routes, axis=1).reshape(group_count, -1) - expert_id).astype(jnp.float32)
    slot_rival = jnp.einsum(
        "bcr,br->bc", expert_table, rival_rows, precision=FULL_PRECISION
    ).reshape(-1)
    partials = lax.cond(
        attention_side, no_inputs, expert_inputs, slot_rows, norm_gain, router, w_gate, w_up
    )
    gate_sum, up_sum, squares, logit_sum = lax.psum(partials, "col")
    hidden = activate(gate_sum, up_sum, squares, logit_sum, slot_rival, expert_id)
    slot_out = lax.cond(attention_side, no_down, expert_down, hidden, w_down)
    returned = jnp.einsum(
        "bcr,bcd->brd",
        expert_table,
        slot_out.reshape(group_count, CAPB, feature_count),
        precision=FULL_PRECISION,
    )
    block_ids = jnp.arange(group_count, dtype=jnp.int32)
    own_pieces = jnp.where(
        (block_ids == group_index)[:, None, None], stream.astype(jnp.float32)[None, :, :], 0.0
    )
    pieces = jnp.where(attention_side, own_pieces, returned)
    outgoing_back = jnp.concatenate([pieces, pieces], axis=0)
    received = lax.all_to_all(
        outgoing_back, ("pool", "grp"), split_axis=0, concat_axis=0, tiled=True
    )
    return jnp.sum(received, axis=0).astype(jnp.bfloat16)

MESH = pl.DeviceIdType.MESH


def fused_kernel(
    queries_hbm,
    fresh_hbm,
    kv_hbm,
    lengths_hbm,
    residual_hbm,
    proj_hbm,
    gain_hbm,
    router_hbm,
    routes_hbm,
    gate_hbm,
    up_hbm,
    down_hbm,
    out,
    queries,
    fresh,
    lengths,
    residual,
    gain,
    router,
    routes,
    kv,
    proj,
    gate_w,
    up_w,
    down_w,
    query_rows,
    key_rows,
    value_rows,
    mixed_own,
    stat_own,
    mixed_in,
    stat_in,
    attended_rows,
    streams,
    sums_own,
    sums_in,
    part_send,
    part_in,
    hidden_own,
    hidden_in,
    pieces,
    returned,
    load_sem,
    weight_sem,
    send_a,
    recv_a,
    send_b,
    recv_b,
    send_c,
    recv_c,
    send_d,
    recv_d,
    send_e,
    recv_e,
    send_f,
    recv_f,
    send_g,
    recv_g,
):
    pools = lax.axis_size("pool")
    groups = lax.axis_size("grp")
    cols = lax.axis_size("col")
    pool = lax.axis_index("pool")
    grp = lax.axis_index("grp")
    col = lax.axis_index("col")
    rows = queries.shape[0]
    positions = kv.shape[1]
    kv_width = KV_HEADS * HEAD_DIM
    group_size = HEADS // KV_HEADS
    chunk = gate_w.shape[2]
    states = rows * HEADS
    first_column = pool * (chunk * cols)

    def col_peer(k):
        return (pool, grp, lax.rem(col + k, cols))

    def row_peer(kp, kg):
        return (lax.rem(pool + kp, pools), lax.rem(grp + kg, groups), col)

    row_steps = [(kp, kg) for kg in range(groups) for kp in range(pools) if kp or kg]
    barrier = pltpu.get_barrier_semaphore()
    for k in range(1, cols):
        pl.semaphore_signal(barrier, inc=1, device_id=col_peer(k), device_id_type=MESH)
    for kp, kg in row_steps:
        pl.semaphore_signal(barrier, inc=1, device_id=row_peer(kp, kg), device_id_type=MESH)

    operands = (
        (queries_hbm, queries),
        (fresh_hbm, fresh),
        (lengths_hbm, lengths),
        (kv_hbm, kv),
        (residual_hbm, residual),
        (gain_hbm, gain),
        (router_hbm, router),
        (routes_hbm, routes),
        (proj_hbm, proj),
    )
    loads = [
        pltpu.make_async_copy(src, dst, load_sem.at[i]) for i, (src, dst) in enumerate(operands)
    ]
    for load in loads:
        load.start()
    steps = list(range(1, cols)) + [0]
    gate_loads, up_loads, down_loads = {}, {}, {}
    for k in steps:
        owner = lax.rem(col + k, cols)
        window = pl.ds(pl.multiple_of(first_column + owner * chunk, 128), chunk)
        gate_loads[k] = pltpu.make_async_copy(
            gate_hbm.at[:, window], gate_w.at[k], weight_sem.at[0, k]
        )
        up_loads[k] = pltpu.make_async_copy(up_hbm.at[:, window], up_w.at[k], weight_sem.at[1, k])
        gate_loads[k].start()
        up_loads[k].start()
    for k in range(cols):
        source = lax.rem(col + cols - k, cols)
        window = pl.ds(pl.multiple_of(first_column + source * chunk, 128), chunk)
        down_loads[k] = pltpu.make_async_copy(
            down_hbm.at[window, :], down_w.at[k], weight_sem.at[2, k]
        )
        down_loads[k].start()

    loads[0].wait()
    loads[1].wait()
    wide_queries = queries[...].astype(jnp.float32)
    wide_fresh = fresh[...].astype(jnp.float32)
    for h in range(HEADS):
        j = h // group_size
        place = pl.ds(h, rows, stride=HEADS)
        query_rows[place, :] = wide_queries[:, h * HEAD_DIM : (h + 1) * HEAD_DIM]
        key_rows[place, :] = wide_fresh[:, j * HEAD_DIM : (j + 1) * HEAD_DIM]
        value_rows[place, :] = wide_fresh[
            :, kv_width + j * HEAD_DIM : kv_width + (j + 1) * HEAD_DIM
        ]
    scale = HEAD_DIM ** (-0.5)
    own_score = jnp.sum(query_rows[...] * key_rows[...], axis=1, keepdims=True) * scale
    head_of = lax.broadcasted_iota(jnp.int32, (HEADS, HEAD_DIM), 0) // group_size
    place = col * positions + lax.broadcasted_iota(jnp.int32, (HEADS, positions), 1)
    loads[2].wait()
    loads[3].wait()
    peaks, totals = [], []
    for r in range(rows):
        head_rows = query_rows[r * HEADS : (r + 1) * HEADS, :]
        spread = jnp.concatenate(
            [jnp.where(head_of == j, head_rows, 0.0) for j in range(KV_HEADS)], axis=1
        ).astype(jnp.bfloat16)
        scores = (
            lax.dot_general(
                spread,
                kv[r, :, :kv_width],
                (((1,), (1,)), ((), ())),
                preferred_element_type=jnp.float32,
            )
            * scale
        )
        valid = place < lengths[r]
        peak = jnp.max(jnp.where(valid, scores, FLOOR_SCORE), axis=1, keepdims=True)
        weights = jnp.where(valid, jnp.exp(scores - peak), 0.0)
        total = jnp.sum(weights, axis=1, keepdims=True)
        high = weights.astype(jnp.bfloat16)
        low = (weights - high.astype(jnp.float32)).astype(jnp.bfloat16)
        values = kv[r, :, kv_width:]
        product = jnp.dot(high, values, preferred_element_type=jnp.float32) + jnp.dot(
            low, values, preferred_element_type=jnp.float32
        )
        mixed = jnp.zeros((HEADS, HEAD_DIM), jnp.float32)
        for j in range(KV_HEADS):
            mixed = mixed + jnp.where(
                head_of == j, product[:, j * HEAD_DIM : (j + 1) * HEAD_DIM], 0.0
            )
        mixed = mixed / jnp.where(total > 0.0, total, 1.0)
        mixed_own[r * HEADS : (r + 1) * HEADS, :] = mixed.astype(jnp.bfloat16)
        peaks.append(peak)
        totals.append(total)
    peak = jnp.concatenate(peaks, axis=0)
    total = jnp.concatenate(totals, axis=0)
    diagonal = lax.broadcasted_iota(jnp.int32, (states, 128), 0) == lax.broadcasted_iota(
        jnp.int32, (states, 128), 1
    )
    stat_own[...] = jnp.zeros_like(stat_own)
    stat_own[0:1, :] = jnp.sum(jnp.where(diagonal, peak, 0.0), axis=0, keepdims=True)
    stat_own[1:2, :] = jnp.sum(jnp.where(diagonal, total, 0.0), axis=0, keepdims=True)

    pl.semaphore_wait(barrier, cols - 1 + len(row_steps))
    state_copies = []
    for k in range(1, cols):
        for src, dst, send, recv in (
            (stat_own, stat_in, send_b, recv_b),
            (mixed_own, mixed_in, send_a, recv_a),
        ):
            copy = pltpu.make_async_remote_copy(
                src_ref=src,
                dst_ref=dst.at[k - 1],
                send_sem=send.at[k - 1],
                recv_sem=recv.at[k - 1],
                device_id=col_peer(k),
                device_id_type=MESH,
            )
            copy.start()
            state_copies.append(copy)
    for copy in state_copies:
        copy.wait_recv()

    all_peaks, all_totals = [peak], [total]
    for k in range(1, cols):
        all_peaks.append(
            jnp.sum(jnp.where(diagonal, stat_in[k - 1, 0:1, :], 0.0), axis=1, keepdims=True)
        )
        all_totals.append(
            jnp.sum(jnp.where(diagonal, stat_in[k - 1, 1:2, :], 0.0), axis=1, keepdims=True)
        )
    top = own_score
    for other in all_peaks:
        top = jnp.maximum(top, other)
    own_weight = jnp.exp(own_score - top)
    weight_sum = own_weight
    mixed_sum = own_weight * value_rows[...]
    for k in range(cols):
        part = mixed_own[...] if k == 0 else mixed_in[k - 1]
        weight = all_totals[k] * jnp.exp(all_peaks[k] - top)
        weight_sum = weight_sum + weight
        mixed_sum = mixed_sum + weight * part.astype(jnp.float32)
    attended_rows[...] = mixed_sum / weight_sum
    attended = jnp.concatenate(
        [attended_rows[pl.ds(h, rows, stride=HEADS), :] for h in range(HEADS)], axis=1
    ).astype(jnp.bfloat16)
    for load in loads[4:]:
        load.wait()
    projected = jnp.dot(attended, proj[...], preferred_element_type=jnp.float32)
    stream = (residual[...].astype(jnp.float32) + projected).astype(jnp.bfloat16)
    pack = streams.shape[1] // rows
    packed_width = streams.shape[2]

    def packed_rows(block):
        return jnp.concatenate(
            [block[:, i * packed_width : (i + 1) * packed_width] for i in range(pack)], axis=0
        ).astype(jnp.bfloat16)

    def unpacked_rows(block):
        return jnp.concatenate([block[i * rows : (i + 1) * rows, :] for i in range(pack)], axis=1)

    streams[grp] = packed_rows(stream.astype(jnp.float32))

    stream_copies = []
    for kg in range(1, groups):
        copy = pltpu.make_async_remote_copy(
            src_ref=streams.at[grp],
            dst_ref=streams.at[grp],
            send_sem=send_c.at[kg - 1],
            recv_sem=recv_c.at[kg - 1],
            device_id=row_peer(0, kg),
            device_id_type=MESH,
        )
        copy.start()
        stream_copies.append(copy)
    for copy in stream_copies:
        copy.wait_recv()

    wide = jnp.concatenate([unpacked_rows(streams[g].astype(jnp.float32)) for g in range(groups)], axis=0)
    scaled = (wide * gain[...]).astype(jnp.bfloat16)
    squares = jnp.sum(wide * wide, axis=1, keepdims=True)
    logit_part = lax.dot_general(
        scaled, router[...], (((1,), (1,)), ((), ())), preferred_element_type=jnp.float32
    )
    lane = lax.broadcasted_iota(jnp.int32, sums_own.shape, 1)
    packed = jnp.where(lane == EXPERTS, squares, 0.0)
    for j in range(EXPERTS):
        packed = packed + jnp.where(lane == j, logit_part[:, j : j + 1], 0.0)
    sums_own[...] = packed
    part_copies = []
    for k in range(1, cols):
        copy = pltpu.make_async_remote_copy(
            src_ref=sums_own,
            dst_ref=sums_in.at[k - 1],
            send_sem=send_d.at[k - 1],
            recv_sem=recv_d.at[k - 1],
            device_id=col_peer(k),
            device_id_type=MESH,
        )
        copy.start()
        part_copies.append(copy)
    row_count = rows * groups
    for k in steps:
        gate_loads[k].wait()
        gate_part = jnp.dot(scaled, gate_w[k], preferred_element_type=jnp.float32)
        up_loads[k].wait()
        up_part = jnp.dot(scaled, up_w[k], preferred_element_type=jnp.float32)
        if k == 0:
            break
        part_send[k - 1, :row_count, :] = gate_part.astype(jnp.bfloat16)
        part_send[k - 1, row_count:, :] = up_part.astype(jnp.bfloat16)
        copy = pltpu.make_async_remote_copy(
            src_ref=part_send.at[k - 1],
            dst_ref=part_in.at[k - 1],
            send_sem=send_e.at[k - 1],
            recv_sem=recv_e.at[k - 1],
            device_id=col_peer(k),
            device_id_type=MESH,
        )
        copy.start()
        part_copies.append(copy)

    for copy in part_copies[: cols - 1]:
        copy.wait_recv()
    sums = sums_own[...]
    for k in range(1, cols):
        sums = sums + sums_in[k - 1]
    inverse = lax.rsqrt(sums[:, EXPERTS : EXPERTS + 1] / D + EPSILON)
    expert = grp // (groups // EXPERTS)
    square = (row_count, row_count)
    row_diagonal = lax.broadcasted_iota(jnp.int32, square, 0) == lax.broadcasted_iota(
        jnp.int32, square, 1
    )
    named = routes[...].astype(jnp.float32)
    first = jnp.sum(jnp.where(row_diagonal, named[0:1, :], 0.0), axis=1, keepdims=True)
    second = jnp.sum(jnp.where(row_diagonal, named[1:2, :], 0.0), axis=1, keepdims=True)
    expert_label = expert.astype(jnp.float32)
    chosen = jnp.logical_or(first == expert_label, second == expert_label)
    rival = first + second - expert_label
    own_logit = jnp.zeros_like(inverse)
    rival_logit = jnp.zeros_like(inverse)
    for j in range(EXPERTS):
        logit = sums[:, j : j + 1] * inverse
        own_logit = own_logit + jnp.where(expert_label == float(j), logit, 0.0)
        rival_logit = rival_logit + jnp.where(rival == float(j), logit, 0.0)
    row_weight = jnp.where(chosen, 1.0 / (1.0 + jnp.exp(rival_logit - own_logit)), 0.0)

    for k in range(1, cols):
        part_copies[cols - 2 + k].wait_recv()
        gate_part = gate_part + part_in[k - 1, :row_count, :].astype(jnp.float32)
        up_part = up_part + part_in[k - 1, row_count:, :].astype(jnp.float32)
    gate = gate_part * inverse
    up = up_part * inverse
    hidden = (gate / (1.0 + jnp.exp(-gate)) * up * row_weight).astype(jnp.bfloat16)
    hidden_own[...] = hidden
    hidden_copies = []
    for k in range(1, cols):
        copy = pltpu.make_async_remote_copy(
            src_ref=hidden_own,
            dst_ref=hidden_in.at[k - 1],
            send_sem=send_f.at[k - 1],
            recv_sem=recv_f.at[k - 1],
            device_id=col_peer(k),
            device_id_type=MESH,
        )
        copy.start()
        hidden_copies.append(copy)
    down_loads[0].wait()
    result = jnp.dot(hidden, down_w[0], preferred_element_type=jnp.float32)
    for k in range(1, cols):
        hidden_copies[k - 1].wait_recv()
        down_loads[k].wait()
        result = result + jnp.dot(hidden_in[k - 1], down_w[k], preferred_element_type=jnp.float32)
    for g in range(groups):
        pieces[g] = packed_rows(result[g * rows : (g + 1) * rows, :])
    me = pool * groups + grp
    returned[me] = pieces[grp]
    piece_copies = []
    for i, (kp, kg) in enumerate(row_steps):
        target = row_peer(kp, kg)
        copy = pltpu.make_async_remote_copy(
            src_ref=pieces.at[target[1]],
            dst_ref=returned.at[me],
            send_sem=send_g.at[i],
            recv_sem=recv_g.at[i],
            device_id=target,
            device_id_type=MESH,
        )
        copy.start()
        piece_copies.append(copy)
    for copy in piece_copies:
        copy.wait_recv()
    final = streams[grp].astype(jnp.float32)
    for i in range(pools * groups):
        final = final + returned[i].astype(jnp.float32)
    out[...] = unpacked_rows(final).astype(jnp.bfloat16)
    for copy in state_copies + stream_copies + part_copies + hidden_copies + piece_copies:
        copy.wait_send()


def fused_local(
    queries,
    fresh_kv,
    kv_cache,
    lengths,
    residual,
    out_proj,
    norm_gain,
    router,
    routes,
    w_gate,
    w_up,
    w_down,
):
    pools, groups, cols = (lax.axis_size(a) for a in ("pool", "grp", "col"))
    rows, features = residual.shape
    row_count = rows * groups
    chunk = w_gate.shape[1] // (pools * cols)
    states = rows * HEADS
    f32, bf16 = jnp.float32, jnp.bfloat16
    packed_shape = (rows * (16 // rows), features // (16 // rows))
    peers = cols - 1
    row_peers = pools * groups - 1
    dma = pltpu.SemaphoreType.DMA
    return pl.pallas_call(
        fused_kernel,
        out_shape=jax.ShapeDtypeStruct((rows, features), bf16),
        in_specs=[pl.BlockSpec(memory_space=pl.ANY)] * 12,
        out_specs=pl.BlockSpec(memory_space=pltpu.VMEM),
        scratch_shapes=[
            pltpu.VMEM(queries.shape, bf16),
            pltpu.VMEM(fresh_kv.shape, bf16),
            pltpu.SMEM(lengths.shape, jnp.int32),
            pltpu.VMEM(residual.shape, bf16),
            pltpu.VMEM((1, features), f32),
            pltpu.VMEM((EXPERTS, features), bf16),
            pltpu.VMEM(routes.shape[::-1], jnp.int32),
            pltpu.VMEM(kv_cache.shape, bf16),
            pltpu.VMEM(out_proj.shape, bf16),
            pltpu.VMEM((cols, features, chunk), bf16),
            pltpu.VMEM((cols, features, chunk), bf16),
            pltpu.VMEM((cols, chunk, features), bf16),
            pltpu.VMEM((states, HEAD_DIM), f32),
            pltpu.VMEM((states, HEAD_DIM), f32),
            pltpu.VMEM((states, HEAD_DIM), f32),
            pltpu.VMEM((states, HEAD_DIM), bf16),
            pltpu.VMEM((8, 128), f32),
            pltpu.VMEM((peers, states, HEAD_DIM), bf16),
            pltpu.VMEM((peers, 8, 128), f32),
            pltpu.VMEM((states, HEAD_DIM), f32),
            pltpu.VMEM((groups,) + packed_shape, bf16),
            pltpu.VMEM((row_count, 128), f32),
            pltpu.VMEM((peers, row_count, 128), f32),
            pltpu.VMEM((peers, 2 * row_count, chunk), bf16),
            pltpu.VMEM((peers, 2 * row_count, chunk), bf16),
            pltpu.VMEM((row_count, chunk), bf16),
            pltpu.VMEM((peers, row_count, chunk), bf16),
            pltpu.VMEM((groups,) + packed_shape, bf16),
            pltpu.VMEM((pools * groups,) + packed_shape, bf16),
            dma((9,)),
            dma((3, cols)),
            dma((peers,)), dma((peers,)),
            dma((peers,)), dma((peers,)),
            dma((groups - 1,)), dma((groups - 1,)),
            dma((peers,)), dma((peers,)),
            dma((peers,)), dma((peers,)),
            dma((peers,)), dma((peers,)),
            dma((row_peers,)), dma((row_peers,)),
        ],
        compiler_params=pltpu.CompilerParams(
            collective_id=0, has_side_effects=True, vmem_limit_bytes=62 * 2**20
        ),
    )(
        queries,
        fresh_kv,
        kv_cache,
        lengths,
        residual,
        out_proj,
        norm_gain.reshape(1, -1),
        router.T,
        routes.T,
        w_gate,
        w_up,
        w_down,
    )


def fits_kernel(mesh, w_gate, residual):
    sizes = dict(mesh.shape)
    chunk, left = divmod(w_gate.shape[1], sizes["grp"] * sizes["pool"] * sizes["col"])
    rows = residual.shape[0] // sizes["grp"]
    states = rows * HEADS
    return (
        left == 0
        and chunk % 128 == 0
        and residual.shape[0] % 16 == 0
        and 16 % rows == 0
        and residual.shape[1] // sizes["col"] % (16 // rows * 128) == 0
        and residual.shape[0] <= 128
        and states <= 128
        and sizes["grp"] % EXPERTS == 0
    )


def solution(mesh):
    placed = (
        P("grp", None),
        P("grp", None),
        P("grp", "col", None),
        P("grp"),
        P("grp", "col"),
        P(None, "col"),
        P("col"),
        P("col", None),
        P(),
        P("col", "grp"),
        P("col", "grp"),
        P("grp", "col"),
    )

    def whole(*args):
        body = fused_local if fits_kernel(mesh, args[9], args[4]) else local
        return jax.shard_map(
            body, mesh=mesh, in_specs=placed, out_specs=P("grp", "col"), check_vma=False
        )(*args)

    return whole
```

```python
import jax
import jax.numpy as jnp
from jax import lax
from jax.experimental import pallas as pl
from jax.experimental.pallas import tpu as pltpu
from jax.sharding import PartitionSpec as P

D = 4096
HEADS = 16
KV_HEADS = 4
HEAD_DIM = 128
EXPERTS = 4
CAPB = 3


EPSILON = 1e-05
FLOOR_SCORE = -1e30
FULL_PRECISION = lax.Precision.HIGHEST


def merged(part, axis, combine):
    gathered = jax.tree.map(lambda a: lax.all_gather(a, axis), part)

    def take(source):
        return jax.tree.map(lambda a: lax.dynamic_index_in_dim(a, source, 0, False), gathered)

    return lax.fori_loop(
        1, lax.axis_size(axis), lambda source, state: combine(state, take(source)), take(0)
    )


def slot_tables(routes, blocks, capacity):
    row_count = routes.shape[0]
    per_block = row_count // blocks
    labels = jnp.arange(EXPERTS, dtype=jnp.int32)
    route_hits = (routes[:, :, None] == labels[None, None, :]).astype(jnp.int32)
    flat_hits = route_hits.reshape(blocks, per_block * 2, EXPERTS)
    earlier = jnp.cumsum(flat_hits, axis=1) - flat_hits
    slot_index = jnp.sum(earlier * flat_hits, axis=2).reshape(blocks, per_block, 2)
    owners = routes.reshape(blocks, per_block, 2)
    expert_hit = (owners[:, :, :, None] == labels[None, None, None, :]).astype(jnp.float32)
    slot_hit = (
        slot_index[:, :, :, None] == jnp.arange(capacity, dtype=jnp.int32)[None, None, None, :]
    ).astype(jnp.float32)
    return jnp.einsum("brke,brkc->becr", expert_hit, slot_hit, precision=FULL_PRECISION)


def attend_block(queries, kv_cache, lengths, first_pos):
    row_count = queries.shape[0]
    group_size = HEADS // KV_HEADS
    kv_width = KV_HEADS * HEAD_DIM
    positions = kv_cache.shape[1]
    query_heads = queries.reshape(row_count, KV_HEADS, group_size, HEAD_DIM)
    key_part = kv_cache[:, :, :kv_width].reshape(row_count, positions, KV_HEADS, HEAD_DIM)
    value_part = (
        kv_cache[:, :, kv_width:]
        .astype(jnp.float32)
        .reshape(row_count, positions, KV_HEADS, HEAD_DIM)
    )
    scores = jnp.einsum(
        "rjgd,rpjd->rjgp", query_heads, key_part, preferred_element_type=jnp.float32
    ) * HEAD_DIM ** (-0.5)
    place = first_pos + jnp.arange(positions, dtype=jnp.int32)
    valid = (place[None, :] < lengths[:, None])[:, None, None, :]
    peak_score = jnp.max(jnp.where(valid, scores, FLOOR_SCORE), axis=3)
    cached_weights = jnp.where(valid, jnp.exp(scores - peak_score[..., None]), 0.0)
    weight_sum = jnp.sum(cached_weights, axis=3)
    mixed_sum = jnp.einsum("rjgp,rpjd->rjgd", cached_weights, value_part, precision=FULL_PRECISION)
    return (
        peak_score.reshape(row_count, HEADS),
        weight_sum.reshape(row_count, HEADS),
        mixed_sum.reshape(row_count, HEADS, HEAD_DIM),
    )


def skip_block(queries, kv_cache, lengths, first_pos):
    row_count = queries.shape[0]
    return (
        jnp.full((row_count, HEADS), FLOOR_SCORE, jnp.float32),
        jnp.zeros((row_count, HEADS), jnp.float32),
        jnp.zeros((row_count, HEADS, HEAD_DIM), jnp.float32),
    )


def merge_states(earlier_state, later_state):
    peak_first, sum_first, mixed_first = earlier_state
    peak_second, sum_second, mixed_second = later_state
    peak_both = jnp.maximum(peak_first, peak_second)
    scale_first = jnp.exp(peak_first - peak_both)
    scale_second = jnp.exp(peak_second - peak_both)
    return (
        peak_both,
        sum_first * scale_first + sum_second * scale_second,
        mixed_first * scale_first[..., None] + mixed_second * scale_second[..., None],
    )


def fold_own(queries, fresh_kv, peak_score, weight_sum, mixed_sum):
    row_count = queries.shape[0]
    group_size = HEADS // KV_HEADS
    kv_width = KV_HEADS * HEAD_DIM
    query_heads = queries.reshape(row_count, KV_HEADS, group_size, HEAD_DIM)
    new_keys = fresh_kv[:, :kv_width].reshape(row_count, KV_HEADS, HEAD_DIM)
    new_values = fresh_kv[:, kv_width:].astype(jnp.float32).reshape(row_count, KV_HEADS, HEAD_DIM)
    own_score = jnp.einsum(
        "rjgd,rjd->rjg", query_heads, new_keys, preferred_element_type=jnp.float32
    ) * HEAD_DIM ** (-0.5)
    own_score = own_score.reshape(row_count, HEADS)
    peak_both = jnp.maximum(peak_score, own_score)
    old_scale = jnp.exp(peak_score - peak_both)
    own_weight = jnp.exp(own_score - peak_both)
    total_weight = weight_sum * old_scale + own_weight
    spread_values = jnp.repeat(new_values, group_size, axis=1)
    mixed_total = mixed_sum * old_scale[..., None] + own_weight[..., None] * spread_values
    return (
        (mixed_total / total_weight[..., None])
        .reshape(row_count, HEADS * HEAD_DIM)
        .astype(jnp.bfloat16)
    )


def expert_inputs(slot_rows, norm_gain, router, w_gate, w_up):
    scaled = (slot_rows.astype(jnp.float32) * norm_gain).astype(jnp.bfloat16)
    gate_part = jnp.dot(scaled, w_gate, preferred_element_type=jnp.float32)
    up_part = jnp.dot(scaled, w_up, preferred_element_type=jnp.float32)
    wide_rows = slot_rows.astype(jnp.float32)
    square_part = jnp.sum(wide_rows * wide_rows, axis=1)
    logit_part = jnp.dot(scaled, router, preferred_element_type=jnp.float32)
    return (gate_part, up_part, square_part, logit_part)


def no_inputs(slot_rows, norm_gain, router, w_gate, w_up):
    slot_count = slot_rows.shape[0]
    return (
        jnp.zeros((slot_count, w_gate.shape[1]), jnp.float32),
        jnp.zeros((slot_count, w_up.shape[1]), jnp.float32),
        jnp.zeros((slot_count,), jnp.float32),
        jnp.zeros((slot_count, router.shape[1]), jnp.float32),
    )


def activate(gate_sum, up_sum, squares, logit_sum, slot_rival, expert_id):
    inverse = lax.rsqrt(squares / D + EPSILON)
    labels = jnp.arange(EXPERTS, dtype=jnp.int32)
    logits = logit_sum * inverse[:, None]
    own_logit = jnp.sum(jnp.where(labels[None, :] == expert_id, logits, 0.0), axis=1)
    rival_logit = jnp.sum(
        jnp.where(labels.astype(jnp.float32)[None, :] == slot_rival[:, None], logits, 0.0), axis=1
    )
    slot_weight = jax.nn.sigmoid(own_logit - rival_logit)
    gate_scaled = gate_sum * inverse[:, None]
    up_scaled = up_sum * inverse[:, None]
    return (jax.nn.silu(gate_scaled) * up_scaled * slot_weight[:, None]).astype(jnp.bfloat16)


def expert_down(hidden, w_down):
    return jnp.dot(hidden, w_down, preferred_element_type=jnp.float32)


def no_down(hidden, w_down):
    return jnp.zeros((hidden.shape[0], w_down.shape[1]), jnp.float32)


def local(
    queries,
    fresh_kv,
    kv_cache,
    lengths,
    residual,
    out_proj,
    norm_gain,
    router,
    routes,
    w_gate,
    w_up,
    w_down,
):
    group_count = lax.axis_size("grp")
    group_index = lax.axis_index("grp")
    col_index = lax.axis_index("col")
    attention_side = lax.axis_index("pool") == 0
    feature_count = residual.shape[1]
    first_pos = col_index * kv_cache.shape[1]
    states = lax.cond(
        attention_side, attend_block, skip_block, queries, kv_cache, lengths, first_pos
    )
    peak_score, weight_sum, mixed_sum = merged(states, "col", merge_states)
    attended = fold_own(queries, fresh_kv, peak_score, weight_sum, mixed_sum)
    projected = jnp.dot(attended, out_proj, preferred_element_type=jnp.float32)
    stream = (residual.astype(jnp.float32) + projected).astype(jnp.bfloat16)
    tables = slot_tables(routes, group_count, CAPB)
    copies = group_count // EXPERTS
    expert_id = group_index // copies
    own_table = lax.dynamic_index_in_dim(tables, group_index, 0, keepdims=False)
    expert_table = lax.dynamic_index_in_dim(tables, expert_id, 1, keepdims=False)
    placed = jnp.einsum(
        "ecr,rd->ecd", own_table.astype(jnp.bfloat16), stream, preferred_element_type=jnp.float32
    )
    filled = jnp.where(
        attention_side,
        jnp.repeat(placed.astype(jnp.bfloat16), copies, axis=0),
        jnp.zeros((group_count, CAPB, feature_count), jnp.bfloat16),
    )
    outgoing = jnp.concatenate([jnp.zeros_like(filled), filled], axis=0)
    gathered = lax.all_to_all(outgoing, ("pool", "grp"), split_axis=0, concat_axis=0, tiled=True)[
        :group_count
    ]
    slot_rows = gathered.reshape(group_count * CAPB, feature_count)
    rival_rows = (jnp.sum(routes, axis=1).reshape(group_count, -1) - expert_id).astype(jnp.float32)
    slot_rival = jnp.einsum(
        "bcr,br->bc", expert_table, rival_rows, precision=FULL_PRECISION
    ).reshape(-1)
    partials = lax.cond(
        attention_side, no_inputs, expert_inputs, slot_rows, norm_gain, router, w_gate, w_up
    )
    gate_sum, up_sum, squares, logit_sum = lax.psum(partials, "col")
    hidden = activate(gate_sum, up_sum, squares, logit_sum, slot_rival, expert_id)
    slot_out = lax.cond(attention_side, no_down, expert_down, hidden, w_down)
    returned = jnp.einsum(
        "bcr,bcd->brd",
        expert_table,
        slot_out.reshape(group_count, CAPB, feature_count),
        precision=FULL_PRECISION,
    )
    block_ids = jnp.arange(group_count, dtype=jnp.int32)
    own_pieces = jnp.where(
        (block_ids == group_index)[:, None, None], stream.astype(jnp.float32)[None, :, :], 0.0
    )
    pieces = jnp.where(attention_side, own_pieces, returned)
    outgoing_back = jnp.concatenate([pieces, pieces], axis=0)
    received = lax.all_to_all(
        outgoing_back, ("pool", "grp"), split_axis=0, concat_axis=0, tiled=True
    )
    return jnp.sum(received, axis=0).astype(jnp.bfloat16)

MESH = pl.DeviceIdType.MESH


def fused_kernel(
    queries_hbm,
    fresh_hbm,
    kv_hbm,
    lengths_hbm,
    residual_hbm,
    proj_hbm,
    gain_hbm,
    router_hbm,
    routes_hbm,
    gate_hbm,
    up_hbm,
    down_hbm,
    out,
    queries,
    fresh,
    lengths,
    residual,
    gain,
    router,
    routes,
    kv,
    proj,
    gate_w,
    up_w,
    down_w,
    query_rows,
    key_rows,
    value_rows,
    mixed_own,
    stat_own,
    mixed_in,
    stat_in,
    attended_rows,
    streams,
    sums_own,
    sums_in,
    part_send,
    part_in,
    hidden_own,
    hidden_in,
    pieces,
    returned,
    load_sem,
    weight_sem,
    send_a,
    recv_a,
    send_b,
    recv_b,
    send_c,
    recv_c,
    send_d,
    recv_d,
    send_e,
    recv_e,
    send_f,
    recv_f,
    send_g,
    recv_g,
):
    pools = lax.axis_size("pool")
    groups = lax.axis_size("grp")
    cols = lax.axis_size("col")
    pool = lax.axis_index("pool")
    grp = lax.axis_index("grp")
    col = lax.axis_index("col")
    rows = queries.shape[0]
    positions = kv.shape[1]
    kv_width = KV_HEADS * HEAD_DIM
    group_size = HEADS // KV_HEADS
    chunk = gate_w.shape[2]
    states = rows * HEADS
    first_column = pool * (chunk * cols)

    def col_peer(k):
        return (pool, grp, lax.rem(col + k, cols))

    def row_peer(kp, kg):
        return (lax.rem(pool + kp, pools), lax.rem(grp + kg, groups), col)

    row_steps = [(kp, kg) for kg in range(groups) for kp in range(pools) if kp or kg]
    barrier = pltpu.get_barrier_semaphore()
    for k in range(1, cols):
        pl.semaphore_signal(barrier, inc=1, device_id=col_peer(k), device_id_type=MESH)
    for kp, kg in row_steps:
        pl.semaphore_signal(barrier, inc=1, device_id=row_peer(kp, kg), device_id_type=MESH)

    operands = (
        (queries_hbm, queries),
        (fresh_hbm, fresh),
        (lengths_hbm, lengths),
        (kv_hbm, kv),
        (residual_hbm, residual),
        (gain_hbm, gain),
        (router_hbm, router),
        (routes_hbm, routes),
        (proj_hbm, proj),
    )
    loads = [
        pltpu.make_async_copy(src, dst, load_sem.at[i]) for i, (src, dst) in enumerate(operands)
    ]
    for load in loads:
        load.start()
    steps = list(range(1, cols)) + [0]
    gate_loads, up_loads, down_loads = {}, {}, {}
    for k in steps:
        owner = lax.rem(col + k, cols)
        window = pl.ds(pl.multiple_of(first_column + owner * chunk, 128), chunk)
        gate_loads[k] = pltpu.make_async_copy(
            gate_hbm.at[:, window], gate_w.at[k], weight_sem.at[0, k]
        )
        up_loads[k] = pltpu.make_async_copy(up_hbm.at[:, window], up_w.at[k], weight_sem.at[1, k])
        gate_loads[k].start(priority=1)
        up_loads[k].start(priority=1)
    for k in range(cols):
        source = lax.rem(col + cols - k, cols)
        window = pl.ds(pl.multiple_of(first_column + source * chunk, 128), chunk)
        down_loads[k] = pltpu.make_async_copy(
            down_hbm.at[window, :], down_w.at[k], weight_sem.at[2, k]
        )

    loads[0].wait()
    loads[1].wait()
    wide_queries = queries[...].astype(jnp.float32)
    wide_fresh = fresh[...].astype(jnp.float32)
    for h in range(HEADS):
        j = h // group_size
        place = pl.ds(h, rows, stride=HEADS)
        query_rows[place, :] = wide_queries[:, h * HEAD_DIM : (h + 1) * HEAD_DIM]
        key_rows[place, :] = wide_fresh[:, j * HEAD_DIM : (j + 1) * HEAD_DIM]
        value_rows[place, :] = wide_fresh[
            :, kv_width + j * HEAD_DIM : kv_width + (j + 1) * HEAD_DIM
        ]
    scale = HEAD_DIM ** (-0.5)
    own_score = jnp.sum(query_rows[...] * key_rows[...], axis=1, keepdims=True) * scale
    head_of = lax.broadcasted_iota(jnp.int32, (HEADS, HEAD_DIM), 0) // group_size
    place = col * positions + lax.broadcasted_iota(jnp.int32, (HEADS, positions), 1)
    loads[2].wait()
    loads[3].wait()
    peaks, totals = [], []
    for r in range(rows):
        head_rows = query_rows[r * HEADS : (r + 1) * HEADS, :]
        spread = jnp.concatenate(
            [jnp.where(head_of == j, head_rows, 0.0) for j in range(KV_HEADS)], axis=1
        ).astype(jnp.bfloat16)
        scores = (
            lax.dot_general(
                spread,
                kv[r, :, :kv_width],
                (((1,), (1,)), ((), ())),
                preferred_element_type=jnp.float32,
            )
            * scale
        )
        valid = place < lengths[r]
        peak = jnp.max(jnp.where(valid, scores, FLOOR_SCORE), axis=1, keepdims=True)
        weights = jnp.where(valid, jnp.exp(scores - peak), 0.0)
        total = jnp.sum(weights, axis=1, keepdims=True)
        high = weights.astype(jnp.bfloat16)
        low = (weights - high.astype(jnp.float32)).astype(jnp.bfloat16)
        values = kv[r, :, kv_width:]
        product = jnp.dot(high, values, preferred_element_type=jnp.float32) + jnp.dot(
            low, values, preferred_element_type=jnp.float32
        )
        mixed = jnp.zeros((HEADS, HEAD_DIM), jnp.float32)
        for j in range(KV_HEADS):
            mixed = mixed + jnp.where(
                head_of == j, product[:, j * HEAD_DIM : (j + 1) * HEAD_DIM], 0.0
            )
        mixed = mixed / jnp.where(total > 0.0, total, 1.0)
        mixed_own[r * HEADS : (r + 1) * HEADS, :] = mixed.astype(jnp.bfloat16)
        peaks.append(peak)
        totals.append(total)
    peak = jnp.concatenate(peaks, axis=0)
    total = jnp.concatenate(totals, axis=0)
    diagonal = lax.broadcasted_iota(jnp.int32, (states, 128), 0) == lax.broadcasted_iota(
        jnp.int32, (states, 128), 1
    )
    stat_own[...] = jnp.zeros_like(stat_own)
    stat_own[0:1, :] = jnp.sum(jnp.where(diagonal, peak, 0.0), axis=0, keepdims=True)
    stat_own[1:2, :] = jnp.sum(jnp.where(diagonal, total, 0.0), axis=0, keepdims=True)

    pl.semaphore_wait(barrier, cols - 1 + len(row_steps))
    state_copies = []
    for k in range(1, cols):
        for src, dst, send, recv in (
            (stat_own, stat_in, send_b, recv_b),
            (mixed_own, mixed_in, send_a, recv_a),
        ):
            copy = pltpu.make_async_remote_copy(
                src_ref=src,
                dst_ref=dst.at[k - 1],
                send_sem=send.at[k - 1],
                recv_sem=recv.at[k - 1],
                device_id=col_peer(k),
                device_id_type=MESH,
            )
            copy.start()
            state_copies.append(copy)
    for copy in state_copies:
        copy.wait_recv()

    all_peaks, all_totals = [peak], [total]
    for k in range(1, cols):
        all_peaks.append(
            jnp.sum(jnp.where(diagonal, stat_in[k - 1, 0:1, :], 0.0), axis=1, keepdims=True)
        )
        all_totals.append(
            jnp.sum(jnp.where(diagonal, stat_in[k - 1, 1:2, :], 0.0), axis=1, keepdims=True)
        )
    top = own_score
    for other in all_peaks:
        top = jnp.maximum(top, other)
    own_weight = jnp.exp(own_score - top)
    weight_sum = own_weight
    mixed_sum = own_weight * value_rows[...]
    for k in range(cols):
        part = mixed_own[...] if k == 0 else mixed_in[k - 1]
        weight = all_totals[k] * jnp.exp(all_peaks[k] - top)
        weight_sum = weight_sum + weight
        mixed_sum = mixed_sum + weight * part.astype(jnp.float32)
    attended_rows[...] = mixed_sum / weight_sum
    attended = jnp.concatenate(
        [attended_rows[pl.ds(h, rows, stride=HEADS), :] for h in range(HEADS)], axis=1
    ).astype(jnp.bfloat16)
    for load in loads[4:]:
        load.wait()
    projected = jnp.dot(attended, proj[...], preferred_element_type=jnp.float32)
    stream = (residual[...].astype(jnp.float32) + projected).astype(jnp.bfloat16)
    pack = streams.shape[1] // rows
    packed_width = streams.shape[2]

    def packed_rows(block):
        return jnp.concatenate(
            [block[:, i * packed_width : (i + 1) * packed_width] for i in range(pack)], axis=0
        ).astype(jnp.bfloat16)

    def unpacked_rows(block):
        return jnp.concatenate([block[i * rows : (i + 1) * rows, :] for i in range(pack)], axis=1)

    streams[grp] = packed_rows(stream.astype(jnp.float32))

    stream_copies = []
    for kg in range(1, groups):
        copy = pltpu.make_async_remote_copy(
            src_ref=streams.at[grp],
            dst_ref=streams.at[grp],
            send_sem=send_c.at[kg - 1],
            recv_sem=recv_c.at[kg - 1],
            device_id=row_peer(0, kg),
            device_id_type=MESH,
        )
        copy.start()
        stream_copies.append(copy)
    for copy in stream_copies:
        copy.wait_recv()

    wide = jnp.concatenate([unpacked_rows(streams[g].astype(jnp.float32)) for g in range(groups)], axis=0)
    scaled = (wide * gain[...]).astype(jnp.bfloat16)
    squares = jnp.sum(wide * wide, axis=1, keepdims=True)
    logit_part = lax.dot_general(
        scaled, router[...], (((1,), (1,)), ((), ())), preferred_element_type=jnp.float32
    )
    lane = lax.broadcasted_iota(jnp.int32, sums_own.shape, 1)
    packed = jnp.where(lane == EXPERTS, squares, 0.0)
    for j in range(EXPERTS):
        packed = packed + jnp.where(lane == j, logit_part[:, j : j + 1], 0.0)
    sums_own[...] = packed
    part_copies = []
    for k in range(1, cols):
        copy = pltpu.make_async_remote_copy(
            src_ref=sums_own,
            dst_ref=sums_in.at[k - 1],
            send_sem=send_d.at[k - 1],
            recv_sem=recv_d.at[k - 1],
            device_id=col_peer(k),
            device_id_type=MESH,
        )
        copy.start()
        part_copies.append(copy)
    row_count = rows * groups
    for k in steps:
        gate_loads[k].wait()
        gate_part = jnp.dot(scaled, gate_w[k], preferred_element_type=jnp.float32)
        up_loads[k].wait()
        up_part = jnp.dot(scaled, up_w[k], preferred_element_type=jnp.float32)
        if k == 0:
            break
        part_send[k - 1, :row_count, :] = gate_part.astype(jnp.bfloat16)
        part_send[k - 1, row_count:, :] = up_part.astype(jnp.bfloat16)
        copy = pltpu.make_async_remote_copy(
            src_ref=part_send.at[k - 1],
            dst_ref=part_in.at[k - 1],
            send_sem=send_e.at[k - 1],
            recv_sem=recv_e.at[k - 1],
            device_id=col_peer(k),
            device_id_type=MESH,
        )
        copy.start()
        part_copies.append(copy)

    for k in range(cols):
        down_loads[k].start()
    for copy in part_copies[: cols - 1]:
        copy.wait_recv()
    sums = sums_own[...]
    for k in range(1, cols):
        sums = sums + sums_in[k - 1]
    inverse = lax.rsqrt(sums[:, EXPERTS : EXPERTS + 1] / D + EPSILON)
    expert = grp // (groups // EXPERTS)
    square = (row_count, row_count)
    row_diagonal = lax.broadcasted_iota(jnp.int32, square, 0) == lax.broadcasted_iota(
        jnp.int32, square, 1
    )
    named = routes[...].astype(jnp.float32)
    first = jnp.sum(jnp.where(row_diagonal, named[0:1, :], 0.0), axis=1, keepdims=True)
    second = jnp.sum(jnp.where(row_diagonal, named[1:2, :], 0.0), axis=1, keepdims=True)
    expert_label = expert.astype(jnp.float32)
    chosen = jnp.logical_or(first == expert_label, second == expert_label)
    rival = first + second - expert_label
    own_logit = jnp.zeros_like(inverse)
    rival_logit = jnp.zeros_like(inverse)
    for j in range(EXPERTS):
        logit = sums[:, j : j + 1] * inverse
        own_logit = own_logit + jnp.where(expert_label == float(j), logit, 0.0)
        rival_logit = rival_logit + jnp.where(rival == float(j), logit, 0.0)
    row_weight = jnp.where(chosen, 1.0 / (1.0 + jnp.exp(rival_logit - own_logit)), 0.0)

    for k in range(1, cols):
        part_copies[cols - 2 + k].wait_recv()
        gate_part = gate_part + part_in[k - 1, :row_count, :].astype(jnp.float32)
        up_part = up_part + part_in[k - 1, row_count:, :].astype(jnp.float32)
    gate = gate_part * inverse
    up = up_part * inverse
    hidden = (gate / (1.0 + jnp.exp(-gate)) * up * row_weight).astype(jnp.bfloat16)
    hidden_own[...] = hidden
    hidden_copies = []
    for k in range(1, cols):
        copy = pltpu.make_async_remote_copy(
            src_ref=hidden_own,
            dst_ref=hidden_in.at[k - 1],
            send_sem=send_f.at[k - 1],
            recv_sem=recv_f.at[k - 1],
            device_id=col_peer(k),
            device_id_type=MESH,
        )
        copy.start()
        hidden_copies.append(copy)
    down_loads[0].wait()
    result = jnp.dot(hidden, down_w[0], preferred_element_type=jnp.float32)
    for k in range(1, cols):
        hidden_copies[k - 1].wait_recv()
        down_loads[k].wait()
        result = result + jnp.dot(hidden_in[k - 1], down_w[k], preferred_element_type=jnp.float32)
    for g in range(groups):
        pieces[g] = packed_rows(result[g * rows : (g + 1) * rows, :])
    me = pool * groups + grp
    returned[me] = pieces[grp]
    piece_copies = []
    for i, (kp, kg) in enumerate(row_steps):
        target = row_peer(kp, kg)
        copy = pltpu.make_async_remote_copy(
            src_ref=pieces.at[target[1]],
            dst_ref=returned.at[me],
            send_sem=send_g.at[i],
            recv_sem=recv_g.at[i],
            device_id=target,
            device_id_type=MESH,
        )
        copy.start()
        piece_copies.append(copy)
    for copy in piece_copies:
        copy.wait_recv()
    final = streams[grp].astype(jnp.float32)
    for i in range(pools * groups):
        final = final + returned[i].astype(jnp.float32)
    out[...] = unpacked_rows(final).astype(jnp.bfloat16)
    for copy in state_copies + stream_copies + part_copies + hidden_copies + piece_copies:
        copy.wait_send()


def fused_local(
    queries,
    fresh_kv,
    kv_cache,
    lengths,
    residual,
    out_proj,
    norm_gain,
    router,
    routes,
    w_gate,
    w_up,
    w_down,
):
    pools, groups, cols = (lax.axis_size(a) for a in ("pool", "grp", "col"))
    rows, features = residual.shape
    row_count = rows * groups
    chunk = w_gate.shape[1] // (pools * cols)
    states = rows * HEADS
    f32, bf16 = jnp.float32, jnp.bfloat16
    packed_shape = (rows * (16 // rows), features // (16 // rows))
    peers = cols - 1
    row_peers = pools * groups - 1
    dma = pltpu.SemaphoreType.DMA
    return pl.pallas_call(
        fused_kernel,
        out_shape=jax.ShapeDtypeStruct((rows, features), bf16),
        in_specs=[pl.BlockSpec(memory_space=pl.ANY)] * 12,
        out_specs=pl.BlockSpec(memory_space=pltpu.VMEM),
        scratch_shapes=[
            pltpu.VMEM(queries.shape, bf16),
            pltpu.VMEM(fresh_kv.shape, bf16),
            pltpu.SMEM(lengths.shape, jnp.int32),
            pltpu.VMEM(residual.shape, bf16),
            pltpu.VMEM((1, features), f32),
            pltpu.VMEM((EXPERTS, features), bf16),
            pltpu.VMEM(routes.shape[::-1], jnp.int32),
            pltpu.VMEM(kv_cache.shape, bf16),
            pltpu.VMEM(out_proj.shape, bf16),
            pltpu.VMEM((cols, features, chunk), bf16),
            pltpu.VMEM((cols, features, chunk), bf16),
            pltpu.VMEM((cols, chunk, features), bf16),
            pltpu.VMEM((states, HEAD_DIM), f32),
            pltpu.VMEM((states, HEAD_DIM), f32),
            pltpu.VMEM((states, HEAD_DIM), f32),
            pltpu.VMEM((states, HEAD_DIM), bf16),
            pltpu.VMEM((8, 128), f32),
            pltpu.VMEM((peers, states, HEAD_DIM), bf16),
            pltpu.VMEM((peers, 8, 128), f32),
            pltpu.VMEM((states, HEAD_DIM), f32),
            pltpu.VMEM((groups,) + packed_shape, bf16),
            pltpu.VMEM((row_count, 128), f32),
            pltpu.VMEM((peers, row_count, 128), f32),
            pltpu.VMEM((peers, 2 * row_count, chunk), bf16),
            pltpu.VMEM((peers, 2 * row_count, chunk), bf16),
            pltpu.VMEM((row_count, chunk), bf16),
            pltpu.VMEM((peers, row_count, chunk), bf16),
            pltpu.VMEM((groups,) + packed_shape, bf16),
            pltpu.VMEM((pools * groups,) + packed_shape, bf16),
            dma((9,)),
            dma((3, cols)),
            dma((peers,)), dma((peers,)),
            dma((peers,)), dma((peers,)),
            dma((groups - 1,)), dma((groups - 1,)),
            dma((peers,)), dma((peers,)),
            dma((peers,)), dma((peers,)),
            dma((peers,)), dma((peers,)),
            dma((row_peers,)), dma((row_peers,)),
        ],
        compiler_params=pltpu.CompilerParams(
            collective_id=0, has_side_effects=True, vmem_limit_bytes=62 * 2**20
        ),
    )(
        queries,
        fresh_kv,
        kv_cache,
        lengths,
        residual,
        out_proj,
        norm_gain.reshape(1, -1),
        router.T,
        routes.T,
        w_gate,
        w_up,
        w_down,
    )


def fits_kernel(mesh, w_gate, residual):
    sizes = dict(mesh.shape)
    chunk, left = divmod(w_gate.shape[1], sizes["grp"] * sizes["pool"] * sizes["col"])
    rows = residual.shape[0] // sizes["grp"]
    states = rows * HEADS
    return (
        left == 0
        and chunk % 128 == 0
        and residual.shape[0] % 16 == 0
        and 16 % rows == 0
        and residual.shape[1] // sizes["col"] % (16 // rows * 128) == 0
        and residual.shape[0] <= 128
        and states <= 128
        and sizes["grp"] % EXPERTS == 0
    )


def solution(mesh):
    placed = (
        P("grp", None),
        P("grp", None),
        P("grp", "col", None),
        P("grp"),
        P("grp", "col"),
        P(None, "col"),
        P("col"),
        P("col", None),
        P(),
        P("col", "grp"),
        P("col", "grp"),
        P("grp", "col"),
    )

    def whole(*args):
        body = fused_local if fits_kernel(mesh, args[9], args[4]) else local
        return jax.shard_map(
            body, mesh=mesh, in_specs=placed, out_specs=P("grp", "col"), check_vma=False
        )(*args)

    return whole
```

```python
import jax
import jax.numpy as jnp
from jax import lax
from jax.experimental import pallas as pl
from jax.experimental.pallas import tpu as pltpu
from jax.sharding import PartitionSpec as P

D = 4096
HEADS = 16
KV_HEADS = 4
HEAD_DIM = 128
EXPERTS = 4
CAPB = 3


EPSILON = 1e-05
FLOOR_SCORE = -1e30
FULL_PRECISION = lax.Precision.HIGHEST


def merged(part, axis, combine):
    gathered = jax.tree.map(lambda a: lax.all_gather(a, axis), part)

    def take(source):
        return jax.tree.map(lambda a: lax.dynamic_index_in_dim(a, source, 0, False), gathered)

    return lax.fori_loop(
        1, lax.axis_size(axis), lambda source, state: combine(state, take(source)), take(0)
    )


def slot_tables(routes, blocks, capacity):
    row_count = routes.shape[0]
    per_block = row_count // blocks
    labels = jnp.arange(EXPERTS, dtype=jnp.int32)
    route_hits = (routes[:, :, None] == labels[None, None, :]).astype(jnp.int32)
    flat_hits = route_hits.reshape(blocks, per_block * 2, EXPERTS)
    earlier = jnp.cumsum(flat_hits, axis=1) - flat_hits
    slot_index = jnp.sum(earlier * flat_hits, axis=2).reshape(blocks, per_block, 2)
    owners = routes.reshape(blocks, per_block, 2)
    expert_hit = (owners[:, :, :, None] == labels[None, None, None, :]).astype(jnp.float32)
    slot_hit = (
        slot_index[:, :, :, None] == jnp.arange(capacity, dtype=jnp.int32)[None, None, None, :]
    ).astype(jnp.float32)
    return jnp.einsum("brke,brkc->becr", expert_hit, slot_hit, precision=FULL_PRECISION)


def attend_block(queries, kv_cache, lengths, first_pos):
    row_count = queries.shape[0]
    group_size = HEADS // KV_HEADS
    kv_width = KV_HEADS * HEAD_DIM
    positions = kv_cache.shape[1]
    query_heads = queries.reshape(row_count, KV_HEADS, group_size, HEAD_DIM)
    key_part = kv_cache[:, :, :kv_width].reshape(row_count, positions, KV_HEADS, HEAD_DIM)
    value_part = (
        kv_cache[:, :, kv_width:]
        .astype(jnp.float32)
        .reshape(row_count, positions, KV_HEADS, HEAD_DIM)
    )
    scores = jnp.einsum(
        "rjgd,rpjd->rjgp", query_heads, key_part, preferred_element_type=jnp.float32
    ) * HEAD_DIM ** (-0.5)
    place = first_pos + jnp.arange(positions, dtype=jnp.int32)
    valid = (place[None, :] < lengths[:, None])[:, None, None, :]
    peak_score = jnp.max(jnp.where(valid, scores, FLOOR_SCORE), axis=3)
    cached_weights = jnp.where(valid, jnp.exp(scores - peak_score[..., None]), 0.0)
    weight_sum = jnp.sum(cached_weights, axis=3)
    mixed_sum = jnp.einsum("rjgp,rpjd->rjgd", cached_weights, value_part, precision=FULL_PRECISION)
    return (
        peak_score.reshape(row_count, HEADS),
        weight_sum.reshape(row_count, HEADS),
        mixed_sum.reshape(row_count, HEADS, HEAD_DIM),
    )


def skip_block(queries, kv_cache, lengths, first_pos):
    row_count = queries.shape[0]
    return (
        jnp.full((row_count, HEADS), FLOOR_SCORE, jnp.float32),
        jnp.zeros((row_count, HEADS), jnp.float32),
        jnp.zeros((row_count, HEADS, HEAD_DIM), jnp.float32),
    )


def merge_states(earlier_state, later_state):
    peak_first, sum_first, mixed_first = earlier_state
    peak_second, sum_second, mixed_second = later_state
    peak_both = jnp.maximum(peak_first, peak_second)
    scale_first = jnp.exp(peak_first - peak_both)
    scale_second = jnp.exp(peak_second - peak_both)
    return (
        peak_both,
        sum_first * scale_first + sum_second * scale_second,
        mixed_first * scale_first[..., None] + mixed_second * scale_second[..., None],
    )


def fold_own(queries, fresh_kv, peak_score, weight_sum, mixed_sum):
    row_count = queries.shape[0]
    group_size = HEADS // KV_HEADS
    kv_width = KV_HEADS * HEAD_DIM
    query_heads = queries.reshape(row_count, KV_HEADS, group_size, HEAD_DIM)
    new_keys = fresh_kv[:, :kv_width].reshape(row_count, KV_HEADS, HEAD_DIM)
    new_values = fresh_kv[:, kv_width:].astype(jnp.float32).reshape(row_count, KV_HEADS, HEAD_DIM)
    own_score = jnp.einsum(
        "rjgd,rjd->rjg", query_heads, new_keys, preferred_element_type=jnp.float32
    ) * HEAD_DIM ** (-0.5)
    own_score = own_score.reshape(row_count, HEADS)
    peak_both = jnp.maximum(peak_score, own_score)
    old_scale = jnp.exp(peak_score - peak_both)
    own_weight = jnp.exp(own_score - peak_both)
    total_weight = weight_sum * old_scale + own_weight
    spread_values = jnp.repeat(new_values, group_size, axis=1)
    mixed_total = mixed_sum * old_scale[..., None] + own_weight[..., None] * spread_values
    return (
        (mixed_total / total_weight[..., None])
        .reshape(row_count, HEADS * HEAD_DIM)
        .astype(jnp.bfloat16)
    )


def expert_inputs(slot_rows, norm_gain, router, w_gate, w_up):
    scaled = (slot_rows.astype(jnp.float32) * norm_gain).astype(jnp.bfloat16)
    gate_part = jnp.dot(scaled, w_gate, preferred_element_type=jnp.float32)
    up_part = jnp.dot(scaled, w_up, preferred_element_type=jnp.float32)
    wide_rows = slot_rows.astype(jnp.float32)
    square_part = jnp.sum(wide_rows * wide_rows, axis=1)
    logit_part = jnp.dot(scaled, router, preferred_element_type=jnp.float32)
    return (gate_part, up_part, square_part, logit_part)


def no_inputs(slot_rows, norm_gain, router, w_gate, w_up):
    slot_count = slot_rows.shape[0]
    return (
        jnp.zeros((slot_count, w_gate.shape[1]), jnp.float32),
        jnp.zeros((slot_count, w_up.shape[1]), jnp.float32),
        jnp.zeros((slot_count,), jnp.float32),
        jnp.zeros((slot_count, router.shape[1]), jnp.float32),
    )


def activate(gate_sum, up_sum, squares, logit_sum, slot_rival, expert_id):
    inverse = lax.rsqrt(squares / D + EPSILON)
    labels = jnp.arange(EXPERTS, dtype=jnp.int32)
    logits = logit_sum * inverse[:, None]
    own_logit = jnp.sum(jnp.where(labels[None, :] == expert_id, logits, 0.0), axis=1)
    rival_logit = jnp.sum(
        jnp.where(labels.astype(jnp.float32)[None, :] == slot_rival[:, None], logits, 0.0), axis=1
    )
    slot_weight = jax.nn.sigmoid(own_logit - rival_logit)
    gate_scaled = gate_sum * inverse[:, None]
    up_scaled = up_sum * inverse[:, None]
    return (jax.nn.silu(gate_scaled) * up_scaled * slot_weight[:, None]).astype(jnp.bfloat16)


def expert_down(hidden, w_down):
    return jnp.dot(hidden, w_down, preferred_element_type=jnp.float32)


def no_down(hidden, w_down):
    return jnp.zeros((hidden.shape[0], w_down.shape[1]), jnp.float32)


def local(
    queries,
    fresh_kv,
    kv_cache,
    lengths,
    residual,
    out_proj,
    norm_gain,
    router,
    routes,
    w_gate,
    w_up,
    w_down,
):
    group_count = lax.axis_size("grp")
    group_index = lax.axis_index("grp")
    col_index = lax.axis_index("col")
    attention_side = lax.axis_index("pool") == 0
    feature_count = residual.shape[1]
    first_pos = col_index * kv_cache.shape[1]
    states = lax.cond(
        attention_side, attend_block, skip_block, queries, kv_cache, lengths, first_pos
    )
    peak_score, weight_sum, mixed_sum = merged(states, "col", merge_states)
    attended = fold_own(queries, fresh_kv, peak_score, weight_sum, mixed_sum)
    projected = jnp.dot(attended, out_proj, preferred_element_type=jnp.float32)
    stream = (residual.astype(jnp.float32) + projected).astype(jnp.bfloat16)
    tables = slot_tables(routes, group_count, CAPB)
    copies = group_count // EXPERTS
    expert_id = group_index // copies
    own_table = lax.dynamic_index_in_dim(tables, group_index, 0, keepdims=False)
    expert_table = lax.dynamic_index_in_dim(tables, expert_id, 1, keepdims=False)
    placed = jnp.einsum(
        "ecr,rd->ecd", own_table.astype(jnp.bfloat16), stream, preferred_element_type=jnp.float32
    )
    filled = jnp.where(
        attention_side,
        jnp.repeat(placed.astype(jnp.bfloat16), copies, axis=0),
        jnp.zeros((group_count, CAPB, feature_count), jnp.bfloat16),
    )
    outgoing = jnp.concatenate([jnp.zeros_like(filled), filled], axis=0)
    gathered = lax.all_to_all(outgoing, ("pool", "grp"), split_axis=0, concat_axis=0, tiled=True)[
        :group_count
    ]
    slot_rows = gathered.reshape(group_count * CAPB, feature_count)
    rival_rows = (jnp.sum(routes, axis=1).reshape(group_count, -1) - expert_id).astype(jnp.float32)
    slot_rival = jnp.einsum(
        "bcr,br->bc", expert_table, rival_rows, precision=FULL_PRECISION
    ).reshape(-1)
    partials = lax.cond(
        attention_side, no_inputs, expert_inputs, slot_rows, norm_gain, router, w_gate, w_up
    )
    gate_sum, up_sum, squares, logit_sum = lax.psum(partials, "col")
    hidden = activate(gate_sum, up_sum, squares, logit_sum, slot_rival, expert_id)
    slot_out = lax.cond(attention_side, no_down, expert_down, hidden, w_down)
    returned = jnp.einsum(
        "bcr,bcd->brd",
        expert_table,
        slot_out.reshape(group_count, CAPB, feature_count),
        precision=FULL_PRECISION,
    )
    block_ids = jnp.arange(group_count, dtype=jnp.int32)
    own_pieces = jnp.where(
        (block_ids == group_index)[:, None, None], stream.astype(jnp.float32)[None, :, :], 0.0
    )
    pieces = jnp.where(attention_side, own_pieces, returned)
    outgoing_back = jnp.concatenate([pieces, pieces], axis=0)
    received = lax.all_to_all(
        outgoing_back, ("pool", "grp"), split_axis=0, concat_axis=0, tiled=True
    )
    return jnp.sum(received, axis=0).astype(jnp.bfloat16)

MESH = pl.DeviceIdType.MESH


def fused_kernel(
    queries_hbm,
    fresh_hbm,
    kv_hbm,
    lengths_hbm,
    residual_hbm,
    proj_hbm,
    gain_hbm,
    router_hbm,
    routes_hbm,
    gate_hbm,
    up_hbm,
    down_hbm,
    out,
    queries,
    fresh,
    lengths,
    residual,
    gain,
    router,
    routes,
    kv,
    proj,
    gate_w,
    up_w,
    down_w,
    query_rows,
    key_rows,
    value_rows,
    mixed_own,
    stat_own,
    mixed_in,
    stat_in,
    attended_rows,
    streams,
    sums_own,
    sums_in,
    part_send,
    part_in,
    hidden_own,
    hidden_in,
    pieces,
    returned,
    load_sem,
    weight_sem,
    send_a,
    recv_a,
    send_b,
    recv_b,
    send_c,
    recv_c,
    send_d,
    recv_d,
    send_e,
    recv_e,
    send_f,
    recv_f,
    send_g,
    recv_g,
):
    pools = lax.axis_size("pool")
    groups = lax.axis_size("grp")
    cols = lax.axis_size("col")
    pool = lax.axis_index("pool")
    grp = lax.axis_index("grp")
    col = lax.axis_index("col")
    rows = queries.shape[0]
    positions = kv.shape[1]
    kv_width = KV_HEADS * HEAD_DIM
    group_size = HEADS // KV_HEADS
    chunk = gate_w.shape[2]
    states = rows * HEADS
    first_column = pool * (chunk * cols)

    def col_peer(k):
        return (pool, grp, lax.rem(col + k, cols))

    def row_peer(kp, kg):
        return (lax.rem(pool + kp, pools), lax.rem(grp + kg, groups), col)

    row_steps = [(kp, kg) for kg in range(groups) for kp in range(pools) if kp or kg]
    barrier = pltpu.get_barrier_semaphore()
    for k in range(1, cols):
        pl.semaphore_signal(barrier, inc=1, device_id=col_peer(k), device_id_type=MESH)
    for kp, kg in row_steps:
        pl.semaphore_signal(barrier, inc=1, device_id=row_peer(kp, kg), device_id_type=MESH)

    operands = (
        (queries_hbm, queries),
        (fresh_hbm, fresh),
        (lengths_hbm, lengths),
        (kv_hbm, kv),
        (residual_hbm, residual),
        (gain_hbm, gain),
        (router_hbm, router),
        (routes_hbm, routes),
        (proj_hbm, proj),
    )
    loads = [
        pltpu.make_async_copy(src, dst, load_sem.at[i]) for i, (src, dst) in enumerate(operands)
    ]
    for load in loads:
        load.start()
    steps = list(range(1, cols)) + [0]
    gate_loads, up_loads, down_loads = {}, {}, {}
    for k in steps:
        owner = lax.rem(col + k, cols)
        window = pl.ds(pl.multiple_of(first_column + owner * chunk, 128), chunk)
        gate_loads[k] = pltpu.make_async_copy(
            gate_hbm.at[:, window], gate_w.at[k], weight_sem.at[0, k]
        )
        up_loads[k] = pltpu.make_async_copy(up_hbm.at[:, window], up_w.at[k], weight_sem.at[1, k])
        gate_loads[k].start(priority=1)
        up_loads[k].start(priority=1)
    for k in range(cols):
        source = lax.rem(col + cols - k, cols)
        window = pl.ds(pl.multiple_of(first_column + source * chunk, 128), chunk)
        down_loads[k] = pltpu.make_async_copy(
            down_hbm.at[window, :], down_w.at[k], weight_sem.at[2, k]
        )

    loads[0].wait()
    loads[1].wait()
    wide_queries = queries[...].astype(jnp.float32)
    wide_fresh = fresh[...].astype(jnp.float32)
    for h in range(HEADS):
        j = h // group_size
        place = pl.ds(h, rows, stride=HEADS)
        query_rows[place, :] = wide_queries[:, h * HEAD_DIM : (h + 1) * HEAD_DIM]
        key_rows[place, :] = wide_fresh[:, j * HEAD_DIM : (j + 1) * HEAD_DIM]
        value_rows[place, :] = wide_fresh[
            :, kv_width + j * HEAD_DIM : kv_width + (j + 1) * HEAD_DIM
        ]
    scale = HEAD_DIM ** (-0.5)
    own_score = jnp.sum(query_rows[...] * key_rows[...], axis=1, keepdims=True) * scale
    head_of = lax.broadcasted_iota(jnp.int32, (HEADS, HEAD_DIM), 0) // group_size
    place = col * positions + lax.broadcasted_iota(jnp.int32, (HEADS, positions), 1)
    loads[2].wait()
    loads[3].wait()
    peaks, totals = [], []
    for r in range(rows):
        head_rows = query_rows[r * HEADS : (r + 1) * HEADS, :]
        spread = jnp.concatenate(
            [jnp.where(head_of == j, head_rows, 0.0) for j in range(KV_HEADS)], axis=1
        ).astype(jnp.bfloat16)
        scores = (
            lax.dot_general(
                spread,
                kv[r, :, :kv_width],
                (((1,), (1,)), ((), ())),
                preferred_element_type=jnp.float32,
            )
            * scale
        )
        valid = place < lengths[r]
        peak = jnp.max(jnp.where(valid, scores, FLOOR_SCORE), axis=1, keepdims=True)
        weights = jnp.where(valid, jnp.exp(scores - peak), 0.0)
        total = jnp.sum(weights, axis=1, keepdims=True)
        high = weights.astype(jnp.bfloat16)
        low = (weights - high.astype(jnp.float32)).astype(jnp.bfloat16)
        values = kv[r, :, kv_width:]
        product = jnp.dot(high, values, preferred_element_type=jnp.float32) + jnp.dot(
            low, values, preferred_element_type=jnp.float32
        )
        mixed = jnp.zeros((HEADS, HEAD_DIM), jnp.float32)
        for j in range(KV_HEADS):
            mixed = mixed + jnp.where(
                head_of == j, product[:, j * HEAD_DIM : (j + 1) * HEAD_DIM], 0.0
            )
        mixed = mixed / jnp.where(total > 0.0, total, 1.0)
        mixed_own[r * HEADS : (r + 1) * HEADS, :] = mixed.astype(jnp.bfloat16)
        peaks.append(peak)
        totals.append(total)
    peak = jnp.concatenate(peaks, axis=0)
    total = jnp.concatenate(totals, axis=0)
    diagonal = lax.broadcasted_iota(jnp.int32, (states, 128), 0) == lax.broadcasted_iota(
        jnp.int32, (states, 128), 1
    )
    stat_own[...] = jnp.zeros_like(stat_own)
    stat_own[0:1, :] = jnp.sum(jnp.where(diagonal, peak, 0.0), axis=0, keepdims=True)
    stat_own[1:2, :] = jnp.sum(jnp.where(diagonal, total, 0.0), axis=0, keepdims=True)

    pl.semaphore_wait(barrier, cols - 1 + len(row_steps))
    state_copies = []
    for k in range(1, cols):
        for src, dst, send, recv in (
            (stat_own, stat_in, send_b, recv_b),
            (mixed_own, mixed_in, send_a, recv_a),
        ):
            copy = pltpu.make_async_remote_copy(
                src_ref=src,
                dst_ref=dst.at[k - 1],
                send_sem=send.at[k - 1],
                recv_sem=recv.at[k - 1],
                device_id=col_peer(k),
                device_id_type=MESH,
            )
            copy.start()
            state_copies.append(copy)
    for copy in state_copies:
        copy.wait_recv()

    all_peaks, all_totals = [peak], [total]
    for k in range(1, cols):
        all_peaks.append(
            jnp.sum(jnp.where(diagonal, stat_in[k - 1, 0:1, :], 0.0), axis=1, keepdims=True)
        )
        all_totals.append(
            jnp.sum(jnp.where(diagonal, stat_in[k - 1, 1:2, :], 0.0), axis=1, keepdims=True)
        )
    top = own_score
    for other in all_peaks:
        top = jnp.maximum(top, other)
    own_weight = jnp.exp(own_score - top)
    weight_sum = own_weight
    mixed_sum = own_weight * value_rows[...]
    for k in range(cols):
        part = mixed_own[...] if k == 0 else mixed_in[k - 1]
        weight = all_totals[k] * jnp.exp(all_peaks[k] - top)
        weight_sum = weight_sum + weight
        mixed_sum = mixed_sum + weight * part.astype(jnp.float32)
    attended_rows[...] = mixed_sum / weight_sum
    attended = jnp.concatenate(
        [attended_rows[pl.ds(h, rows, stride=HEADS), :] for h in range(HEADS)], axis=1
    ).astype(jnp.bfloat16)
    for load in loads[4:]:
        load.wait()
    projected = jnp.dot(attended, proj[...], preferred_element_type=jnp.float32)
    stream = (residual[...].astype(jnp.float32) + projected).astype(jnp.bfloat16)
    pack = streams.shape[1] // rows
    packed_width = streams.shape[2]

    def packed_rows(block):
        return jnp.concatenate(
            [block[:, i * packed_width : (i + 1) * packed_width] for i in range(pack)], axis=0
        ).astype(jnp.bfloat16)

    def unpacked_rows(block):
        return jnp.concatenate([block[i * rows : (i + 1) * rows, :] for i in range(pack)], axis=1)

    streams[grp] = packed_rows(stream.astype(jnp.float32))

    stream_copies = []
    for kg in range(1, groups):
        copy = pltpu.make_async_remote_copy(
            src_ref=streams.at[grp],
            dst_ref=streams.at[grp],
            send_sem=send_c.at[kg - 1],
            recv_sem=recv_c.at[kg - 1],
            device_id=row_peer(0, kg),
            device_id_type=MESH,
        )
        copy.start()
        stream_copies.append(copy)
    row_count = rows * groups
    slots = CAPB * groups
    expert_label = (grp // (groups // EXPERTS)).astype(jnp.float32)
    square = (row_count, row_count)
    down_index = lax.broadcasted_iota(jnp.int32, square, 0)
    across_index = lax.broadcasted_iota(jnp.int32, square, 1)
    named = routes[...].astype(jnp.float32)
    first, second = named[0:1, :], named[1:2, :]
    hit_row = jnp.where(first == expert_label, 1.0, 0.0) + jnp.where(
        second == expert_label, 1.0, 0.0
    )
    hit_col = jnp.sum(jnp.where(down_index == across_index, hit_row, 0.0), axis=1, keepdims=True)
    rank_row = jnp.sum(jnp.where(down_index < across_index, hit_col, 0.0), axis=0, keepdims=True)
    rank_col = jnp.sum(jnp.where(across_index < down_index, hit_row, 0.0), axis=1, keepdims=True)
    to_slots = jnp.where(down_index.astype(jnp.float32) == rank_row, hit_row, 0.0)
    to_rows = jnp.where(across_index.astype(jnp.float32) == rank_col, hit_col, 0.0)
    filled = jnp.sum(to_slots, axis=1, keepdims=True) > 0.5
    rival = jnp.sum(to_slots * (first + second - expert_label), axis=1, keepdims=True)
    for copy in stream_copies:
        copy.wait_recv()

    wide = jnp.concatenate([unpacked_rows(streams[g].astype(jnp.float32)) for g in range(groups)], axis=0)
    wide = jnp.dot(
        to_slots.astype(jnp.bfloat16),
        wide.astype(jnp.bfloat16),
        preferred_element_type=jnp.float32,
    )
    scaled = (wide * gain[...]).astype(jnp.bfloat16)
    squares = jnp.sum(wide * wide, axis=1, keepdims=True)
    logit_part = lax.dot_general(
        scaled, router[...], (((1,), (1,)), ((), ())), preferred_element_type=jnp.float32
    )
    lane = lax.broadcasted_iota(jnp.int32, sums_own.shape, 1)
    packed = jnp.where(lane == EXPERTS, squares, 0.0)
    for j in range(EXPERTS):
        packed = packed + jnp.where(lane == j, logit_part[:, j : j + 1], 0.0)
    sums_own[...] = packed
    part_copies = []
    for k in range(1, cols):
        copy = pltpu.make_async_remote_copy(
            src_ref=sums_own,
            dst_ref=sums_in.at[k - 1],
            send_sem=send_d.at[k - 1],
            recv_sem=recv_d.at[k - 1],
            device_id=col_peer(k),
            device_id_type=MESH,
        )
        copy.start()
        part_copies.append(copy)
    side = part_send.shape[2] - chunk
    extra = slots - 8

    def packed_parts(gate, up):
        rest = jnp.concatenate([gate[8:slots, :], up[8:slots, :]], axis=0)
        rest = jnp.concatenate([rest, jnp.zeros((8, 2 * side - chunk), jnp.float32)], axis=1)
        return jnp.concatenate(
            [
                jnp.concatenate([gate[:8, :], rest[:, :side]], axis=1),
                jnp.concatenate([up[:8, :], rest[:, side:]], axis=1),
            ],
            axis=0,
        )

    for k in steps:
        gate_loads[k].wait()
        gate_part = jnp.dot(scaled, gate_w[k], preferred_element_type=jnp.float32)
        up_loads[k].wait()
        up_part = jnp.dot(scaled, up_w[k], preferred_element_type=jnp.float32)
        if k == 0:
            break
        part_send[k - 1] = packed_parts(gate_part, up_part).astype(jnp.bfloat16)
        copy = pltpu.make_async_remote_copy(
            src_ref=part_send.at[k - 1],
            dst_ref=part_in.at[k - 1],
            send_sem=send_e.at[k - 1],
            recv_sem=recv_e.at[k - 1],
            device_id=col_peer(k),
            device_id_type=MESH,
        )
        copy.start()
        part_copies.append(copy)

    for k in range(cols):
        down_loads[k].start()
    for copy in part_copies[: cols - 1]:
        copy.wait_recv()
    total_part = packed_parts(gate_part, up_part)
    sums = sums_own[...]
    for k in range(1, cols):
        sums = sums + sums_in[k - 1]
    inverse = lax.rsqrt(sums[:, EXPERTS : EXPERTS + 1] / D + EPSILON)
    own_logit = jnp.zeros_like(inverse)
    rival_logit = jnp.zeros_like(inverse)
    for j in range(EXPERTS):
        logit = sums[:, j : j + 1] * inverse
        own_logit = own_logit + jnp.where(expert_label == float(j), logit, 0.0)
        rival_logit = rival_logit + jnp.where(rival == float(j), logit, 0.0)
    row_weight = jnp.where(filled, 1.0 / (1.0 + jnp.exp(rival_logit - own_logit)), 0.0)

    for k in range(1, cols):
        part_copies[cols - 2 + k].wait_recv()
        total_part = total_part + part_in[k - 1].astype(jnp.float32)
    rest = jnp.concatenate([total_part[:8, chunk:], total_part[8:, chunk:]], axis=1)[:, :chunk]
    blank = jnp.zeros((row_count - slots, chunk), jnp.float32)
    gate_part = jnp.concatenate([total_part[:8, :chunk], rest[:extra, :], blank], axis=0)
    up_part = jnp.concatenate([total_part[8:, :chunk], rest[extra:, :], blank], axis=0)
    gate = gate_part * inverse
    up = up_part * inverse
    hidden = (gate / (1.0 + jnp.exp(-gate)) * up * row_weight).astype(jnp.bfloat16)
    hidden_own[...] = hidden
    hidden_copies = []
    for k in range(1, cols):
        copy = pltpu.make_async_remote_copy(
            src_ref=hidden_own,
            dst_ref=hidden_in.at[k - 1],
            send_sem=send_f.at[k - 1],
            recv_sem=recv_f.at[k - 1],
            device_id=col_peer(k),
            device_id_type=MESH,
        )
        copy.start()
        hidden_copies.append(copy)
    down_loads[0].wait()
    result = jnp.dot(hidden, down_w[0], preferred_element_type=jnp.float32)
    for k in range(1, cols):
        hidden_copies[k - 1].wait_recv()
        down_loads[k].wait()
        result = result + jnp.dot(hidden_in[k - 1], down_w[k], preferred_element_type=jnp.float32)
    result = jnp.dot(
        to_rows.astype(jnp.bfloat16),
        result.astype(jnp.bfloat16),
        preferred_element_type=jnp.float32,
    )
    for g in range(groups):
        pieces[g] = packed_rows(result[g * rows : (g + 1) * rows, :])
    me = pool * groups + grp
    returned[me] = pieces[grp]
    piece_copies = []
    for i, (kp, kg) in enumerate(row_steps):
        target = row_peer(kp, kg)
        copy = pltpu.make_async_remote_copy(
            src_ref=pieces.at[target[1]],
            dst_ref=returned.at[me],
            send_sem=send_g.at[i],
            recv_sem=recv_g.at[i],
            device_id=target,
            device_id_type=MESH,
        )
        copy.start()
        piece_copies.append(copy)
    for copy in piece_copies:
        copy.wait_recv()
    final = streams[grp].astype(jnp.float32)
    for i in range(pools * groups):
        final = final + returned[i].astype(jnp.float32)
    out[...] = unpacked_rows(final).astype(jnp.bfloat16)
    for copy in state_copies + stream_copies + part_copies + hidden_copies + piece_copies:
        copy.wait_send()


def fused_local(
    queries,
    fresh_kv,
    kv_cache,
    lengths,
    residual,
    out_proj,
    norm_gain,
    router,
    routes,
    w_gate,
    w_up,
    w_down,
):
    pools, groups, cols = (lax.axis_size(a) for a in ("pool", "grp", "col"))
    rows, features = residual.shape
    row_count = rows * groups
    chunk = w_gate.shape[1] // (pools * cols)
    states = rows * HEADS
    f32, bf16 = jnp.float32, jnp.bfloat16
    packed_shape = (rows * (16 // rows), features // (16 // rows))
    peers = cols - 1
    row_peers = pools * groups - 1
    dma = pltpu.SemaphoreType.DMA
    return pl.pallas_call(
        fused_kernel,
        out_shape=jax.ShapeDtypeStruct((rows, features), bf16),
        in_specs=[pl.BlockSpec(memory_space=pl.ANY)] * 12,
        out_specs=pl.BlockSpec(memory_space=pltpu.VMEM),
        scratch_shapes=[
            pltpu.VMEM(queries.shape, bf16),
            pltpu.VMEM(fresh_kv.shape, bf16),
            pltpu.SMEM(lengths.shape, jnp.int32),
            pltpu.VMEM(residual.shape, bf16),
            pltpu.VMEM((1, features), f32),
            pltpu.VMEM((EXPERTS, features), bf16),
            pltpu.VMEM(routes.shape[::-1], jnp.int32),
            pltpu.VMEM(kv_cache.shape, bf16),
            pltpu.VMEM(out_proj.shape, bf16),
            pltpu.VMEM((cols, features, chunk), bf16),
            pltpu.VMEM((cols, features, chunk), bf16),
            pltpu.VMEM((cols, chunk, features), bf16),
            pltpu.VMEM((states, HEAD_DIM), f32),
            pltpu.VMEM((states, HEAD_DIM), f32),
            pltpu.VMEM((states, HEAD_DIM), f32),
            pltpu.VMEM((states, HEAD_DIM), bf16),
            pltpu.VMEM((8, 128), f32),
            pltpu.VMEM((peers, states, HEAD_DIM), bf16),
            pltpu.VMEM((peers, 8, 128), f32),
            pltpu.VMEM((states, HEAD_DIM), f32),
            pltpu.VMEM((groups,) + packed_shape, bf16),
            pltpu.VMEM((row_count, 128), f32),
            pltpu.VMEM((peers, row_count, 128), f32),
            pltpu.VMEM((peers, 16, chunk + (chunk + 255) // 256 * 128), bf16),
            pltpu.VMEM((peers, 16, chunk + (chunk + 255) // 256 * 128), bf16),
            pltpu.VMEM((row_count, chunk), bf16),
            pltpu.VMEM((peers, row_count, chunk), bf16),
            pltpu.VMEM((groups,) + packed_shape, bf16),
            pltpu.VMEM((pools * groups,) + packed_shape, bf16),
            dma((9,)),
            dma((3, cols)),
            dma((peers,)), dma((peers,)),
            dma((peers,)), dma((peers,)),
            dma((groups - 1,)), dma((groups - 1,)),
            dma((peers,)), dma((peers,)),
            dma((peers,)), dma((peers,)),
            dma((peers,)), dma((peers,)),
            dma((row_peers,)), dma((row_peers,)),
        ],
        compiler_params=pltpu.CompilerParams(
            collective_id=0, has_side_effects=True, vmem_limit_bytes=62 * 2**20
        ),
    )(
        queries,
        fresh_kv,
        kv_cache,
        lengths,
        residual,
        out_proj,
        norm_gain.reshape(1, -1),
        router.T,
        routes.T,
        w_gate,
        w_up,
        w_down,
    )


def fits_kernel(mesh, w_gate, residual):
    sizes = dict(mesh.shape)
    chunk, left = divmod(w_gate.shape[1], sizes["grp"] * sizes["pool"] * sizes["col"])
    rows = residual.shape[0] // sizes["grp"]
    states = rows * HEADS
    return (
        left == 0
        and chunk % 128 == 0
        and residual.shape[0] == 16
        and CAPB * sizes["grp"] == 12
        and 16 % rows == 0
        and residual.shape[1] // sizes["col"] % (16 // rows * 128) == 0
        and states <= 128
        and sizes["grp"] % EXPERTS == 0
    )


def solution(mesh):
    placed = (
        P("grp", None),
        P("grp", None),
        P("grp", "col", None),
        P("grp"),
        P("grp", "col"),
        P(None, "col"),
        P("col"),
        P("col", None),
        P(),
        P("col", "grp"),
        P("col", "grp"),
        P("grp", "col"),
    )

    def whole(*args):
        body = fused_local if fits_kernel(mesh, args[9], args[4]) else local
        return jax.shard_map(
            body, mesh=mesh, in_specs=placed, out_specs=P("grp", "col"), check_vma=False
        )(*args)

    return whole
```

```python
import jax
import jax.numpy as jnp
from jax import lax
from jax.experimental import pallas as pl
from jax.experimental.pallas import tpu as pltpu
from jax.sharding import PartitionSpec as P

D = 4096
HEADS = 16
KV_HEADS = 4
HEAD_DIM = 128
EXPERTS = 4
CAPB = 3


EPSILON = 1e-05
FLOOR_SCORE = -1e30
FULL_PRECISION = lax.Precision.HIGHEST


def merged(part, axis, combine):
    gathered = jax.tree.map(lambda a: lax.all_gather(a, axis), part)

    def take(source):
        return jax.tree.map(lambda a: lax.dynamic_index_in_dim(a, source, 0, False), gathered)

    return lax.fori_loop(
        1, lax.axis_size(axis), lambda source, state: combine(state, take(source)), take(0)
    )


def slot_tables(routes, blocks, capacity):
    row_count = routes.shape[0]
    per_block = row_count // blocks
    labels = jnp.arange(EXPERTS, dtype=jnp.int32)
    route_hits = (routes[:, :, None] == labels[None, None, :]).astype(jnp.int32)
    flat_hits = route_hits.reshape(blocks, per_block * 2, EXPERTS)
    earlier = jnp.cumsum(flat_hits, axis=1) - flat_hits
    slot_index = jnp.sum(earlier * flat_hits, axis=2).reshape(blocks, per_block, 2)
    owners = routes.reshape(blocks, per_block, 2)
    expert_hit = (owners[:, :, :, None] == labels[None, None, None, :]).astype(jnp.float32)
    slot_hit = (
        slot_index[:, :, :, None] == jnp.arange(capacity, dtype=jnp.int32)[None, None, None, :]
    ).astype(jnp.float32)
    return jnp.einsum("brke,brkc->becr", expert_hit, slot_hit, precision=FULL_PRECISION)


def attend_block(queries, kv_cache, lengths, first_pos):
    row_count = queries.shape[0]
    group_size = HEADS // KV_HEADS
    kv_width = KV_HEADS * HEAD_DIM
    positions = kv_cache.shape[1]
    query_heads = queries.reshape(row_count, KV_HEADS, group_size, HEAD_DIM)
    key_part = kv_cache[:, :, :kv_width].reshape(row_count, positions, KV_HEADS, HEAD_DIM)
    value_part = (
        kv_cache[:, :, kv_width:]
        .astype(jnp.float32)
        .reshape(row_count, positions, KV_HEADS, HEAD_DIM)
    )
    scores = jnp.einsum(
        "rjgd,rpjd->rjgp", query_heads, key_part, preferred_element_type=jnp.float32
    ) * HEAD_DIM ** (-0.5)
    place = first_pos + jnp.arange(positions, dtype=jnp.int32)
    valid = (place[None, :] < lengths[:, None])[:, None, None, :]
    peak_score = jnp.max(jnp.where(valid, scores, FLOOR_SCORE), axis=3)
    cached_weights = jnp.where(valid, jnp.exp(scores - peak_score[..., None]), 0.0)
    weight_sum = jnp.sum(cached_weights, axis=3)
    mixed_sum = jnp.einsum("rjgp,rpjd->rjgd", cached_weights, value_part, precision=FULL_PRECISION)
    return (
        peak_score.reshape(row_count, HEADS),
        weight_sum.reshape(row_count, HEADS),
        mixed_sum.reshape(row_count, HEADS, HEAD_DIM),
    )


def skip_block(queries, kv_cache, lengths, first_pos):
    row_count = queries.shape[0]
    return (
        jnp.full((row_count, HEADS), FLOOR_SCORE, jnp.float32),
        jnp.zeros((row_count, HEADS), jnp.float32),
        jnp.zeros((row_count, HEADS, HEAD_DIM), jnp.float32),
    )


def merge_states(earlier_state, later_state):
    peak_first, sum_first, mixed_first = earlier_state
    peak_second, sum_second, mixed_second = later_state
    peak_both = jnp.maximum(peak_first, peak_second)
    scale_first = jnp.exp(peak_first - peak_both)
    scale_second = jnp.exp(peak_second - peak_both)
    return (
        peak_both,
        sum_first * scale_first + sum_second * scale_second,
        mixed_first * scale_first[..., None] + mixed_second * scale_second[..., None],
    )


def fold_own(queries, fresh_kv, peak_score, weight_sum, mixed_sum):
    row_count = queries.shape[0]
    group_size = HEADS // KV_HEADS
    kv_width = KV_HEADS * HEAD_DIM
    query_heads = queries.reshape(row_count, KV_HEADS, group_size, HEAD_DIM)
    new_keys = fresh_kv[:, :kv_width].reshape(row_count, KV_HEADS, HEAD_DIM)
    new_values = fresh_kv[:, kv_width:].astype(jnp.float32).reshape(row_count, KV_HEADS, HEAD_DIM)
    own_score = jnp.einsum(
        "rjgd,rjd->rjg", query_heads, new_keys, preferred_element_type=jnp.float32
    ) * HEAD_DIM ** (-0.5)
    own_score = own_score.reshape(row_count, HEADS)
    peak_both = jnp.maximum(peak_score, own_score)
    old_scale = jnp.exp(peak_score - peak_both)
    own_weight = jnp.exp(own_score - peak_both)
    total_weight = weight_sum * old_scale + own_weight
    spread_values = jnp.repeat(new_values, group_size, axis=1)
    mixed_total = mixed_sum * old_scale[..., None] + own_weight[..., None] * spread_values
    return (
        (mixed_total / total_weight[..., None])
        .reshape(row_count, HEADS * HEAD_DIM)
        .astype(jnp.bfloat16)
    )


def expert_inputs(slot_rows, norm_gain, router, w_gate, w_up):
    scaled = (slot_rows.astype(jnp.float32) * norm_gain).astype(jnp.bfloat16)
    gate_part = jnp.dot(scaled, w_gate, preferred_element_type=jnp.float32)
    up_part = jnp.dot(scaled, w_up, preferred_element_type=jnp.float32)
    wide_rows = slot_rows.astype(jnp.float32)
    square_part = jnp.sum(wide_rows * wide_rows, axis=1)
    logit_part = jnp.dot(scaled, router, preferred_element_type=jnp.float32)
    return (gate_part, up_part, square_part, logit_part)


def no_inputs(slot_rows, norm_gain, router, w_gate, w_up):
    slot_count = slot_rows.shape[0]
    return (
        jnp.zeros((slot_count, w_gate.shape[1]), jnp.float32),
        jnp.zeros((slot_count, w_up.shape[1]), jnp.float32),
        jnp.zeros((slot_count,), jnp.float32),
        jnp.zeros((slot_count, router.shape[1]), jnp.float32),
    )


def activate(gate_sum, up_sum, squares, logit_sum, slot_rival, expert_id):
    inverse = lax.rsqrt(squares / D + EPSILON)
    labels = jnp.arange(EXPERTS, dtype=jnp.int32)
    logits = logit_sum * inverse[:, None]
    own_logit = jnp.sum(jnp.where(labels[None, :] == expert_id, logits, 0.0), axis=1)
    rival_logit = jnp.sum(
        jnp.where(labels.astype(jnp.float32)[None, :] == slot_rival[:, None], logits, 0.0), axis=1
    )
    slot_weight = jax.nn.sigmoid(own_logit - rival_logit)
    gate_scaled = gate_sum * inverse[:, None]
    up_scaled = up_sum * inverse[:, None]
    return (jax.nn.silu(gate_scaled) * up_scaled * slot_weight[:, None]).astype(jnp.bfloat16)


def expert_down(hidden, w_down):
    return jnp.dot(hidden, w_down, preferred_element_type=jnp.float32)


def no_down(hidden, w_down):
    return jnp.zeros((hidden.shape[0], w_down.shape[1]), jnp.float32)


def local(
    queries,
    fresh_kv,
    kv_cache,
    lengths,
    residual,
    out_proj,
    norm_gain,
    router,
    routes,
    w_gate,
    w_up,
    w_down,
):
    group_count = lax.axis_size("grp")
    group_index = lax.axis_index("grp")
    col_index = lax.axis_index("col")
    attention_side = lax.axis_index("pool") == 0
    feature_count = residual.shape[1]
    first_pos = col_index * kv_cache.shape[1]
    states = lax.cond(
        attention_side, attend_block, skip_block, queries, kv_cache, lengths, first_pos
    )
    peak_score, weight_sum, mixed_sum = merged(states, "col", merge_states)
    attended = fold_own(queries, fresh_kv, peak_score, weight_sum, mixed_sum)
    projected = jnp.dot(attended, out_proj, preferred_element_type=jnp.float32)
    stream = (residual.astype(jnp.float32) + projected).astype(jnp.bfloat16)
    tables = slot_tables(routes, group_count, CAPB)
    copies = group_count // EXPERTS
    expert_id = group_index // copies
    own_table = lax.dynamic_index_in_dim(tables, group_index, 0, keepdims=False)
    expert_table = lax.dynamic_index_in_dim(tables, expert_id, 1, keepdims=False)
    placed = jnp.einsum(
        "ecr,rd->ecd", own_table.astype(jnp.bfloat16), stream, preferred_element_type=jnp.float32
    )
    filled = jnp.where(
        attention_side,
        jnp.repeat(placed.astype(jnp.bfloat16), copies, axis=0),
        jnp.zeros((group_count, CAPB, feature_count), jnp.bfloat16),
    )
    outgoing = jnp.concatenate([jnp.zeros_like(filled), filled], axis=0)
    gathered = lax.all_to_all(outgoing, ("pool", "grp"), split_axis=0, concat_axis=0, tiled=True)[
        :group_count
    ]
    slot_rows = gathered.reshape(group_count * CAPB, feature_count)
    rival_rows = (jnp.sum(routes, axis=1).reshape(group_count, -1) - expert_id).astype(jnp.float32)
    slot_rival = jnp.einsum(
        "bcr,br->bc", expert_table, rival_rows, precision=FULL_PRECISION
    ).reshape(-1)
    partials = lax.cond(
        attention_side, no_inputs, expert_inputs, slot_rows, norm_gain, router, w_gate, w_up
    )
    gate_sum, up_sum, squares, logit_sum = lax.psum(partials, "col")
    hidden = activate(gate_sum, up_sum, squares, logit_sum, slot_rival, expert_id)
    slot_out = lax.cond(attention_side, no_down, expert_down, hidden, w_down)
    returned = jnp.einsum(
        "bcr,bcd->brd",
        expert_table,
        slot_out.reshape(group_count, CAPB, feature_count),
        precision=FULL_PRECISION,
    )
    block_ids = jnp.arange(group_count, dtype=jnp.int32)
    own_pieces = jnp.where(
        (block_ids == group_index)[:, None, None], stream.astype(jnp.float32)[None, :, :], 0.0
    )
    pieces = jnp.where(attention_side, own_pieces, returned)
    outgoing_back = jnp.concatenate([pieces, pieces], axis=0)
    received = lax.all_to_all(
        outgoing_back, ("pool", "grp"), split_axis=0, concat_axis=0, tiled=True
    )
    return jnp.sum(received, axis=0).astype(jnp.bfloat16)

MESH = pl.DeviceIdType.MESH


def fused_kernel(
    queries_hbm,
    fresh_hbm,
    kv_hbm,
    lengths_hbm,
    residual_hbm,
    proj_hbm,
    gain_hbm,
    router_hbm,
    routes_hbm,
    gate_hbm,
    up_hbm,
    down_hbm,
    out,
    queries,
    fresh,
    lengths,
    residual,
    gain,
    router,
    routes,
    kv,
    proj,
    gate_w,
    up_w,
    down_w,
    query_rows,
    key_rows,
    value_rows,
    mixed_own,
    stat_own,
    mixed_in,
    stat_in,
    attended_rows,
    streams,
    sums_own,
    sums_in,
    part_send,
    part_in,
    hidden_own,
    hidden_in,
    pieces,
    returned,
    load_sem,
    weight_sem,
    send_a,
    recv_a,
    send_b,
    recv_b,
    send_c,
    recv_c,
    send_d,
    recv_d,
    send_e,
    recv_e,
    send_f,
    recv_f,
    send_g,
    recv_g,
):
    pools = lax.axis_size("pool")
    groups = lax.axis_size("grp")
    cols = lax.axis_size("col")
    pool = lax.axis_index("pool")
    grp = lax.axis_index("grp")
    col = lax.axis_index("col")
    rows = queries.shape[0]
    positions = kv.shape[1]
    kv_width = KV_HEADS * HEAD_DIM
    group_size = HEADS // KV_HEADS
    chunk = gate_w.shape[2]
    states = rows * HEADS
    first_column = pool * (chunk * cols)

    def col_peer(k):
        return (pool, grp, lax.rem(col + k, cols))

    def row_peer(kp, kg):
        return (lax.rem(pool + kp, pools), lax.rem(grp + kg, groups), col)

    row_steps = [(kp, kg) for kg in range(groups) for kp in range(pools) if kp or kg]
    barrier = pltpu.get_barrier_semaphore()
    for k in range(1, cols):
        pl.semaphore_signal(barrier, inc=1, device_id=col_peer(k), device_id_type=MESH)
    for kp, kg in row_steps:
        pl.semaphore_signal(barrier, inc=1, device_id=row_peer(kp, kg), device_id_type=MESH)

    operands = (
        (queries_hbm, queries),
        (fresh_hbm, fresh),
        (lengths_hbm, lengths),
        (kv_hbm, kv),
        (residual_hbm, residual),
        (gain_hbm, gain),
        (router_hbm, router),
        (routes_hbm, routes),
        (proj_hbm, proj),
    )
    loads = [
        pltpu.make_async_copy(src, dst, load_sem.at[i]) for i, (src, dst) in enumerate(operands)
    ]
    for load in loads:
        load.start()
    steps = [cols // 2] + [k for k in range(1, cols) if k != cols // 2] + [0]
    gate_loads, up_loads, down_loads = {}, {}, {}
    for k in steps:
        owner = lax.rem(col + k, cols)
        window = pl.ds(pl.multiple_of(first_column + owner * chunk, 128), chunk)
        gate_loads[k] = pltpu.make_async_copy(
            gate_hbm.at[:, window], gate_w.at[k], weight_sem.at[0, k]
        )
        up_loads[k] = pltpu.make_async_copy(up_hbm.at[:, window], up_w.at[k], weight_sem.at[1, k])
        gate_loads[k].start(priority=1)
        up_loads[k].start(priority=1)
    for k in range(cols):
        source = lax.rem(col + cols - k, cols)
        window = pl.ds(pl.multiple_of(first_column + source * chunk, 128), chunk)
        down_loads[k] = pltpu.make_async_copy(
            down_hbm.at[window, :], down_w.at[k], weight_sem.at[2, k]
        )

    loads[0].wait()
    loads[1].wait()
    wide_queries = queries[...].astype(jnp.float32)
    wide_fresh = fresh[...].astype(jnp.float32)
    for h in range(HEADS):
        j = h // group_size
        place = pl.ds(h, rows, stride=HEADS)
        query_rows[place, :] = wide_queries[:, h * HEAD_DIM : (h + 1) * HEAD_DIM]
        key_rows[place, :] = wide_fresh[:, j * HEAD_DIM : (j + 1) * HEAD_DIM]
        value_rows[place, :] = wide_fresh[
            :, kv_width + j * HEAD_DIM : kv_width + (j + 1) * HEAD_DIM
        ]
    scale = HEAD_DIM ** (-0.5)
    own_score = jnp.sum(query_rows[...] * key_rows[...], axis=1, keepdims=True) * scale
    head_of = lax.broadcasted_iota(jnp.int32, (HEADS, HEAD_DIM), 0) // group_size
    place = col * positions + lax.broadcasted_iota(jnp.int32, (HEADS, positions), 1)
    loads[2].wait()
    loads[3].wait()
    peaks, totals = [], []
    for r in range(rows):
        head_rows = query_rows[r * HEADS : (r + 1) * HEADS, :]
        spread = jnp.concatenate(
            [jnp.where(head_of == j, head_rows, 0.0) for j in range(KV_HEADS)], axis=1
        ).astype(jnp.bfloat16)
        scores = (
            lax.dot_general(
                spread,
                kv[r, :, :kv_width],
                (((1,), (1,)), ((), ())),
                preferred_element_type=jnp.float32,
            )
            * scale
        )
        valid = place < lengths[r]
        peak = jnp.max(jnp.where(valid, scores, FLOOR_SCORE), axis=1, keepdims=True)
        weights = jnp.where(valid, jnp.exp(scores - peak), 0.0)
        total = jnp.sum(weights, axis=1, keepdims=True)
        high = weights.astype(jnp.bfloat16)
        low = (weights - high.astype(jnp.float32)).astype(jnp.bfloat16)
        values = kv[r, :, kv_width:]
        product = jnp.dot(high, values, preferred_element_type=jnp.float32) + jnp.dot(
            low, values, preferred_element_type=jnp.float32
        )
        mixed = jnp.zeros((HEADS, HEAD_DIM), jnp.float32)
        for j in range(KV_HEADS):
            mixed = mixed + jnp.where(
                head_of == j, product[:, j * HEAD_DIM : (j + 1) * HEAD_DIM], 0.0
            )
        mixed = mixed / jnp.where(total > 0.0, total, 1.0)
        mixed_own[r * HEADS : (r + 1) * HEADS, :] = mixed.astype(jnp.bfloat16)
        peaks.append(peak)
        totals.append(total)
    peak = jnp.concatenate(peaks, axis=0)
    total = jnp.concatenate(totals, axis=0)
    diagonal = lax.broadcasted_iota(jnp.int32, (states, 128), 0) == lax.broadcasted_iota(
        jnp.int32, (states, 128), 1
    )
    stat_own[...] = jnp.zeros_like(stat_own)
    stat_own[0:1, :] = jnp.sum(jnp.where(diagonal, peak, 0.0), axis=0, keepdims=True)
    stat_own[1:2, :] = jnp.sum(jnp.where(diagonal, total, 0.0), axis=0, keepdims=True)

    pl.semaphore_wait(barrier, cols - 1 + len(row_steps))
    state_copies = []
    for k in range(1, cols):
        for src, dst, send, recv in (
            (stat_own, stat_in, send_b, recv_b),
            (mixed_own, mixed_in, send_a, recv_a),
        ):
            copy = pltpu.make_async_remote_copy(
                src_ref=src,
                dst_ref=dst.at[k - 1],
                send_sem=send.at[k - 1],
                recv_sem=recv.at[k - 1],
                device_id=col_peer(k),
                device_id_type=MESH,
            )
            copy.start()
            state_copies.append(copy)
    for copy in state_copies:
        copy.wait_recv()

    all_peaks, all_totals = [peak], [total]
    for k in range(1, cols):
        all_peaks.append(
            jnp.sum(jnp.where(diagonal, stat_in[k - 1, 0:1, :], 0.0), axis=1, keepdims=True)
        )
        all_totals.append(
            jnp.sum(jnp.where(diagonal, stat_in[k - 1, 1:2, :], 0.0), axis=1, keepdims=True)
        )
    top = own_score
    for other in all_peaks:
        top = jnp.maximum(top, other)
    own_weight = jnp.exp(own_score - top)
    weight_sum = own_weight
    mixed_sum = own_weight * value_rows[...]
    for k in range(cols):
        part = mixed_own[...] if k == 0 else mixed_in[k - 1]
        weight = all_totals[k] * jnp.exp(all_peaks[k] - top)
        weight_sum = weight_sum + weight
        mixed_sum = mixed_sum + weight * part.astype(jnp.float32)
    attended_rows[...] = mixed_sum / weight_sum
    attended = jnp.concatenate(
        [attended_rows[pl.ds(h, rows, stride=HEADS), :] for h in range(HEADS)], axis=1
    ).astype(jnp.bfloat16)
    for load in loads[4:]:
        load.wait()
    projected = jnp.dot(attended, proj[...], preferred_element_type=jnp.float32)
    stream = (residual[...].astype(jnp.float32) + projected).astype(jnp.bfloat16)
    pack = streams.shape[1] // rows
    packed_width = streams.shape[2]

    def packed_rows(block):
        return jnp.concatenate(
            [block[:, i * packed_width : (i + 1) * packed_width] for i in range(pack)], axis=0
        ).astype(jnp.bfloat16)

    def unpacked_rows(block):
        return jnp.concatenate([block[i * rows : (i + 1) * rows, :] for i in range(pack)], axis=1)

    streams[grp] = packed_rows(stream.astype(jnp.float32))

    stream_copies = []
    for kg in range(1, groups):
        copy = pltpu.make_async_remote_copy(
            src_ref=streams.at[grp],
            dst_ref=streams.at[grp],
            send_sem=send_c.at[kg - 1],
            recv_sem=recv_c.at[kg - 1],
            device_id=row_peer(0, kg),
            device_id_type=MESH,
        )
        copy.start()
        stream_copies.append(copy)
    row_count = rows * groups
    slots = CAPB * groups
    expert_label = (grp // (groups // EXPERTS)).astype(jnp.float32)
    square = (row_count, row_count)
    down_index = lax.broadcasted_iota(jnp.int32, square, 0)
    across_index = lax.broadcasted_iota(jnp.int32, square, 1)
    named = routes[...].astype(jnp.float32)
    first, second = named[0:1, :], named[1:2, :]
    hit_row = jnp.where(first == expert_label, 1.0, 0.0) + jnp.where(
        second == expert_label, 1.0, 0.0
    )
    hit_col = jnp.sum(jnp.where(down_index == across_index, hit_row, 0.0), axis=1, keepdims=True)
    rank_row = jnp.sum(jnp.where(down_index < across_index, hit_col, 0.0), axis=0, keepdims=True)
    rank_col = jnp.sum(jnp.where(across_index < down_index, hit_row, 0.0), axis=1, keepdims=True)
    to_slots = jnp.where(down_index.astype(jnp.float32) == rank_row, hit_row, 0.0)
    to_rows = jnp.where(across_index.astype(jnp.float32) == rank_col, hit_col, 0.0)
    filled = jnp.sum(to_slots, axis=1, keepdims=True) > 0.5
    rival = jnp.sum(to_slots * (first + second - expert_label), axis=1, keepdims=True)
    for copy in stream_copies:
        copy.wait_recv()

    wide = jnp.concatenate([unpacked_rows(streams[g].astype(jnp.float32)) for g in range(groups)], axis=0)
    wide = jnp.dot(
        to_slots.astype(jnp.bfloat16),
        wide.astype(jnp.bfloat16),
        preferred_element_type=jnp.float32,
    )
    scaled = (wide * gain[...]).astype(jnp.bfloat16)
    squares = jnp.sum(wide * wide, axis=1, keepdims=True)
    logit_part = lax.dot_general(
        scaled, router[...], (((1,), (1,)), ((), ())), preferred_element_type=jnp.float32
    )
    lane = lax.broadcasted_iota(jnp.int32, sums_own.shape, 1)
    packed = jnp.where(lane == EXPERTS, squares, 0.0)
    for j in range(EXPERTS):
        packed = packed + jnp.where(lane == j, logit_part[:, j : j + 1], 0.0)
    sums_own[...] = packed
    part_copies = []
    for k in range(1, cols):
        copy = pltpu.make_async_remote_copy(
            src_ref=sums_own,
            dst_ref=sums_in.at[k - 1],
            send_sem=send_d.at[k - 1],
            recv_sem=recv_d.at[k - 1],
            device_id=col_peer(k),
            device_id_type=MESH,
        )
        copy.start()
        part_copies.append(copy)
    side = part_send.shape[2] - chunk
    extra = slots - 8

    def packed_parts(gate, up):
        rest = jnp.concatenate([gate[8:slots, :], up[8:slots, :]], axis=0)
        rest = jnp.concatenate([rest, jnp.zeros((8, 2 * side - chunk), jnp.float32)], axis=1)
        return jnp.concatenate(
            [
                jnp.concatenate([gate[:8, :], rest[:, :side]], axis=1),
                jnp.concatenate([up[:8, :], rest[:, side:]], axis=1),
            ],
            axis=0,
        )

    for k in steps:
        gate_loads[k].wait()
        gate_part = jnp.dot(scaled, gate_w[k], preferred_element_type=jnp.float32)
        up_loads[k].wait()
        up_part = jnp.dot(scaled, up_w[k], preferred_element_type=jnp.float32)
        if k == 0:
            break
        part_send[k - 1] = packed_parts(gate_part, up_part).astype(jnp.bfloat16)
        copy = pltpu.make_async_remote_copy(
            src_ref=part_send.at[k - 1],
            dst_ref=part_in.at[k - 1],
            send_sem=send_e.at[k - 1],
            recv_sem=recv_e.at[k - 1],
            device_id=col_peer(k),
            device_id_type=MESH,
        )
        copy.start()
        part_copies.append(copy)

    for k in range(cols):
        down_loads[k].start()
    for copy in part_copies[: cols - 1]:
        copy.wait_recv()
    total_part = packed_parts(gate_part, up_part)
    sums = sums_own[...]
    for k in range(1, cols):
        sums = sums + sums_in[k - 1]
    inverse = lax.rsqrt(sums[:, EXPERTS : EXPERTS + 1] / D + EPSILON)
    own_logit = jnp.zeros_like(inverse)
    rival_logit = jnp.zeros_like(inverse)
    for j in range(EXPERTS):
        logit = sums[:, j : j + 1] * inverse
        own_logit = own_logit + jnp.where(expert_label == float(j), logit, 0.0)
        rival_logit = rival_logit + jnp.where(rival == float(j), logit, 0.0)
    row_weight = jnp.where(filled, 1.0 / (1.0 + jnp.exp(rival_logit - own_logit)), 0.0)

    for i, k in enumerate(steps[:-1]):
        part_copies[cols - 1 + i].wait_recv()
        total_part = total_part + part_in[k - 1].astype(jnp.float32)
    rest = jnp.concatenate([total_part[:8, chunk:], total_part[8:, chunk:]], axis=1)[:, :chunk]
    blank = jnp.zeros((row_count - slots, chunk), jnp.float32)
    gate_part = jnp.concatenate([total_part[:8, :chunk], rest[:extra, :], blank], axis=0)
    up_part = jnp.concatenate([total_part[8:, :chunk], rest[extra:, :], blank], axis=0)
    gate = gate_part * inverse
    up = up_part * inverse
    hidden = (gate / (1.0 + jnp.exp(-gate)) * up * row_weight).astype(jnp.bfloat16)
    hidden_own[...] = hidden
    hidden_copies = []
    for k in range(1, cols):
        copy = pltpu.make_async_remote_copy(
            src_ref=hidden_own,
            dst_ref=hidden_in.at[k - 1],
            send_sem=send_f.at[k - 1],
            recv_sem=recv_f.at[k - 1],
            device_id=col_peer(k),
            device_id_type=MESH,
        )
        copy.start()
        hidden_copies.append(copy)
    down_loads[0].wait()
    result = jnp.dot(hidden, down_w[0], preferred_element_type=jnp.float32)
    for k in range(1, cols):
        hidden_copies[k - 1].wait_recv()
        down_loads[k].wait()
        result = result + jnp.dot(hidden_in[k - 1], down_w[k], preferred_element_type=jnp.float32)
    result = jnp.dot(
        to_rows.astype(jnp.bfloat16),
        result.astype(jnp.bfloat16),
        preferred_element_type=jnp.float32,
    )
    for g in range(groups):
        pieces[g] = packed_rows(result[g * rows : (g + 1) * rows, :])
    me = pool * groups + grp
    returned[me] = pieces[grp]
    piece_copies = []
    for i, (kp, kg) in enumerate(row_steps):
        target = row_peer(kp, kg)
        copy = pltpu.make_async_remote_copy(
            src_ref=pieces.at[target[1]],
            dst_ref=returned.at[me],
            send_sem=send_g.at[i],
            recv_sem=recv_g.at[i],
            device_id=target,
            device_id_type=MESH,
        )
        copy.start()
        piece_copies.append(copy)
    for copy in piece_copies:
        copy.wait_recv()
    final = streams[grp].astype(jnp.float32)
    for i in range(pools * groups):
        final = final + returned[i].astype(jnp.float32)
    out[...] = unpacked_rows(final).astype(jnp.bfloat16)
    for copy in state_copies + stream_copies + part_copies + hidden_copies + piece_copies:
        copy.wait_send()


def fused_local(
    queries,
    fresh_kv,
    kv_cache,
    lengths,
    residual,
    out_proj,
    norm_gain,
    router,
    routes,
    w_gate,
    w_up,
    w_down,
):
    pools, groups, cols = (lax.axis_size(a) for a in ("pool", "grp", "col"))
    rows, features = residual.shape
    row_count = rows * groups
    chunk = w_gate.shape[1] // (pools * cols)
    states = rows * HEADS
    f32, bf16 = jnp.float32, jnp.bfloat16
    packed_shape = (rows * (16 // rows), features // (16 // rows))
    peers = cols - 1
    row_peers = pools * groups - 1
    dma = pltpu.SemaphoreType.DMA
    return pl.pallas_call(
        fused_kernel,
        out_shape=jax.ShapeDtypeStruct((rows, features), bf16),
        in_specs=[pl.BlockSpec(memory_space=pl.ANY)] * 12,
        out_specs=pl.BlockSpec(memory_space=pltpu.VMEM),
        scratch_shapes=[
            pltpu.VMEM(queries.shape, bf16),
            pltpu.VMEM(fresh_kv.shape, bf16),
            pltpu.SMEM(lengths.shape, jnp.int32),
            pltpu.VMEM(residual.shape, bf16),
            pltpu.VMEM((1, features), f32),
            pltpu.VMEM((EXPERTS, features), bf16),
            pltpu.VMEM(routes.shape[::-1], jnp.int32),
            pltpu.VMEM(kv_cache.shape, bf16),
            pltpu.VMEM(out_proj.shape, bf16),
            pltpu.VMEM((cols, features, chunk), bf16),
            pltpu.VMEM((cols, features, chunk), bf16),
            pltpu.VMEM((cols, chunk, features), bf16),
            pltpu.VMEM((states, HEAD_DIM), f32),
            pltpu.VMEM((states, HEAD_DIM), f32),
            pltpu.VMEM((states, HEAD_DIM), f32),
            pltpu.VMEM((states, HEAD_DIM), bf16),
            pltpu.VMEM((8, 128), f32),
            pltpu.VMEM((peers, states, HEAD_DIM), bf16),
            pltpu.VMEM((peers, 8, 128), f32),
            pltpu.VMEM((states, HEAD_DIM), f32),
            pltpu.VMEM((groups,) + packed_shape, bf16),
            pltpu.VMEM((row_count, 128), f32),
            pltpu.VMEM((peers, row_count, 128), f32),
            pltpu.VMEM((peers, 16, chunk + (chunk + 255) // 256 * 128), bf16),
            pltpu.VMEM((peers, 16, chunk + (chunk + 255) // 256 * 128), bf16),
            pltpu.VMEM((row_count, chunk), bf16),
            pltpu.VMEM((peers, row_count, chunk), bf16),
            pltpu.VMEM((groups,) + packed_shape, bf16),
            pltpu.VMEM((pools * groups,) + packed_shape, bf16),
            dma((9,)),
            dma((3, cols)),
            dma((peers,)), dma((peers,)),
            dma((peers,)), dma((peers,)),
            dma((groups - 1,)), dma((groups - 1,)),
            dma((peers,)), dma((peers,)),
            dma((peers,)), dma((peers,)),
            dma((peers,)), dma((peers,)),
            dma((row_peers,)), dma((row_peers,)),
        ],
        compiler_params=pltpu.CompilerParams(
            collective_id=0, has_side_effects=True, vmem_limit_bytes=62 * 2**20
        ),
    )(
        queries,
        fresh_kv,
        kv_cache,
        lengths,
        residual,
        out_proj,
        norm_gain.reshape(1, -1),
        router.T,
        routes.T,
        w_gate,
        w_up,
        w_down,
    )


def fits_kernel(mesh, w_gate, residual):
    sizes = dict(mesh.shape)
    chunk, left = divmod(w_gate.shape[1], sizes["grp"] * sizes["pool"] * sizes["col"])
    rows = residual.shape[0] // sizes["grp"]
    states = rows * HEADS
    return (
        left == 0
        and chunk % 128 == 0
        and residual.shape[0] == 16
        and CAPB * sizes["grp"] == 12
        and 16 % rows == 0
        and residual.shape[1] // sizes["col"] % (16 // rows * 128) == 0
        and states <= 128
        and sizes["grp"] % EXPERTS == 0
    )


def solution(mesh):
    placed = (
        P("grp", None),
        P("grp", None),
        P("grp", "col", None),
        P("grp"),
        P("grp", "col"),
        P(None, "col"),
        P("col"),
        P("col", None),
        P(),
        P("col", "grp"),
        P("col", "grp"),
        P("grp", "col"),
    )

    def whole(*args):
        body = fused_local if fits_kernel(mesh, args[9], args[4]) else local
        return jax.shard_map(
            body, mesh=mesh, in_specs=placed, out_specs=P("grp", "col"), check_vma=False
        )(*args)

    return whole
```
